32 devices in a mesh: group: 2 (over x), patch: 16 (over z, y, core).
Axes of the slice: x: 2, y: 2, z: 4, core: 2. Of those that a mesh axis runs over, the one named last changes fastest.
Arguments:
- img_hidden: bfloat16 [2304, 3072], P(('group', 'patch')), parts along dimension 0, may hold values from -6 to 6
- img_qkv: bfloat16 [2304, 4608], P(('group', 'patch')), parts along dimension 0, may hold values from -6 to 6
- stale_kv: bfloat16 [2, 2304, 1536], P(None, ('group', 'patch')), parts along dimension 1, may hold values from -68 to 68
- txt_hidden: bfloat16 [64, 3072], P('group', 'patch'), parts along dimension 0, may hold values from -6 to 6
- txt_qkv: bfloat16 [64, 4608], P('group'), parts along dimension 0, may hold values from -6 to 6
- txt_mask: int32 [64], P('group'), parts along dimension 0, may hold values 0 or 1
- img_qk_gain: float32 [2, 128], replicated, may hold values from 0.1 to 1.9
- txt_qk_gain: float32 [2, 128], replicated, may hold values from 0.1 to 1.9
- img_gate: float32 [6144], P('group'), parts along dimension 0, may hold values from -4 to 4
- txt_gate: float32 [6144], P(('group', 'patch')), parts along dimension 0, may hold values from -4 to 4
- img_out_w: bfloat16 [1536, 3072], replicated, may hold values from -0.15625 to 0.15625
- txt_out_w: bfloat16 [1536, 3072], P(None, 'patch'), may hold values from -0.15625 to 0.15625
Outputs:
- img_out: bfloat16 [2304, 3072], P(('group', 'patch')), parts along dimension 0
- txt_out: bfloat16 [64, 3072], P('group', 'patch'), parts along dimension 0
- fresh_kv: bfloat16 [2, 2304, 1536], P(None, ('group', 'patch')), parts along dimension 1
The draws below stay inside these ranges and needn't reach their ends.
There are 2 independent parts, one for each index of `group`. The reference program is written for one: setup_inputs(seed, part) draws one part's arguments, and reference() takes and returns one part's arrays. A program takes and returns all parts, laid end to end along the dimension named above; an argument that names none is the same for every part. Nothing has to cross between parts.
All inputs are finite; a program needn't handle non-finite values.
Results may differ from the reference program's by a relative error of at most 0.011.
Values may be sent and summed in bfloat16 or wider, within the bound.
A program may use at most 256 MiB of HBM per device.

```python
import math
import jax
import jax.numpy as jnp
from jax import lax

D = 3072
HEADS = 12
HD = 128
TOK_DEV = 72
TXT = 32
HW = 1536
IMG = 1152
N_PATCH = 16


def draw_stale_kv(key, part):
    key = jax.random.fold_in(key, 11)
    base = jnp.clip(jax.random.normal(key, (2, IMG, HW)), -6.0, 6.0)
    return base.astype(jnp.bfloat16)


def place_ends(drawn, stream_key, low, high):
    longest = drawn.shape.index(max(drawn.shape))
    spots = []
    for shift in (0, 1):
        where = [jax.random.randint(jax.random.fold_in(stream_key, axis), (), 0, length) for axis, length in enumerate(drawn.shape)]
        where[longest] = (where[longest] + shift) % drawn.shape[longest]
        spots.append(tuple(where))
    return drawn.at[spots[0]].set(low).at[spots[1]].set(high)


def shard_levels(rng, extent, shards, least, top_value):
    loudness, own = 1.0, jax.random.fold_in(rng, 6)
    for position, blocks in shards:
        draws = jnp.exp(jax.random.uniform(jax.random.fold_in(own, position), (blocks,), jnp.float32, least / len(shards), top_value / len(shards)))
        loudness = loudness * jnp.repeat(draws, extent[position] // blocks).reshape([-1 if axis == position else 1 for axis in range(len(extent))])
    return loudness


def bell_draw(key, shape, scale, most, cuts=(), held_as=jnp.bfloat16):
    drawn = scale * jax.random.normal(key, shape, jnp.float32)
    if cuts:
        drawn = drawn * shard_levels(key, shape, cuts, -0.22, 0.18)
    return jnp.clip(drawn, -most, most).astype(held_as)


def setup_inputs(seed: int = 0, part: int = 0) -> dict:
    seeds = jax.random.split(jax.random.key(seed), 13)
    part_splits = jax.random.split(jax.random.fold_in(seeds[12], part), 13)
    return {
        "img_hidden": bell_draw(part_splits[0], (IMG, D), 1.0, 6.0, ((0, 16),)),
        "img_qkv": bell_draw(part_splits[1], (IMG, 3 * HW), 1.0, 6.0, ((0, 16),)),
        "stale_kv": draw_stale_kv(jax.random.fold_in(jax.random.fold_in(seeds[12], part), 71), part),
        "txt_hidden": bell_draw(part_splits[3], (TXT, D), 1.0, 6.0, ((1, 16),)),
        "txt_qkv": bell_draw(part_splits[4], (TXT, 3 * HW), 1.0, 6.0),
        "txt_mask": place_ends((jax.random.randint(part_splits[5], (TXT,), 0, 4) < 3).astype(jnp.int32), jax.random.fold_in(part_splits[5], 1), 0, 1),
        "img_qk_gain": jnp.clip(1.0 + 0.18 * jax.random.normal(seeds[6], (2, HD), jnp.float32), 0.1, 1.9),
        "txt_qk_gain": jnp.clip(1.0 + 0.18 * jax.random.normal(seeds[7], (2, HD), jnp.float32), 0.1, 1.9),
        "img_gate": bell_draw(part_splits[8], (D,), 1.0, 4.0, (), jnp.float32),
        "txt_gate": bell_draw(part_splits[9], (D,), 1.0, 4.0, ((0, 16),), jnp.float32),
        "img_out_w": bell_draw(seeds[10], (HW, D), HW ** -0.5, 0.15625),
        "txt_out_w": bell_draw(seeds[11], (HW, D), HW ** -0.5, 0.15625, ((1, 16),)),
    }


def head_norm(block, gain):
    lead = block.shape[0]
    split = block.reshape(lead, HEADS, HD)
    scaled = split * lax.rsqrt(lax.optimization_barrier(jnp.mean(split * split, axis=-1, keepdims=True)) + 1e-06) * gain
    return scaled.reshape(lead, HEADS * HD)

def prepare(qkv, gains):
    width = HEADS * HD
    raw = qkv.astype(jnp.float32)
    query = head_norm(raw[:, :width], gains[0]).astype(jnp.bfloat16)
    keys = head_norm(raw[:, width:2 * width], gains[1]).astype(jnp.bfloat16)
    values = qkv[:, 2 * width:]
    return (query, keys, values)

def attend(query, keys, values, valid):
    rows = query.shape[0]
    count = keys.shape[0]
    q_three = query.astype(jnp.float32).reshape(rows, HEADS, HD)
    k_three = keys.astype(jnp.float32).reshape(count, HEADS, HD)
    v_three = values.astype(jnp.float32).reshape(count, HEADS, HD)
    scores = jnp.einsum('rhd,khd->rhk', q_three, k_three) * (1.0 / math.sqrt(HD))
    scores = jnp.where(valid[None, None, :], scores, -jnp.inf)
    highest = lax.optimization_barrier(jnp.max(scores, axis=-1, keepdims=True))
    weights = jnp.exp(scores - highest)
    total = lax.optimization_barrier(jnp.sum(weights, axis=-1))
    rounded = lax.optimization_barrier(weights.astype(jnp.bfloat16))
    mixed = jnp.einsum('rhk,khd->rhd', rounded.astype(jnp.float32), v_three)
    return (mixed / total[..., None]).astype(jnp.bfloat16).reshape(rows, HEADS * HD)

def reference(img_hidden, img_qkv, stale_kv, txt_hidden, txt_qkv, txt_mask, img_qk_gain, txt_qk_gain, img_gate, txt_gate, img_out_w, txt_out_w):
    img_q, img_k, img_v = prepare(img_qkv, img_qk_gain)
    txt_q, txt_k, txt_v = prepare(txt_qkv, txt_qk_gain)
    fresh_kv = jnp.stack([img_k, img_v])
    txt_valid = txt_mask == 1
    all_video = jnp.ones((IMG,), dtype=bool)
    slab_of = jnp.arange(IMG, dtype=jnp.int32) // TOK_DEV

    def one_slab(index):
        query = lax.dynamic_slice_in_dim(img_q, (index * TOK_DEV).astype(jnp.int32), TOK_DEV, 0)
        own = (slab_of == index)[:, None]
        keys = jnp.where(own, img_k, stale_kv[0])
        values = jnp.where(own, img_v, stale_kv[1])
        return attend(query, jnp.concatenate([txt_k, keys]), jnp.concatenate([txt_v, values]), jnp.concatenate([txt_valid, all_video]))
    img_attn = lax.map(one_slab, jnp.arange(N_PATCH, dtype=jnp.int32)).reshape(IMG, HEADS * HD)
    txt_attn = attend(txt_q, jnp.concatenate([txt_k, img_k]), jnp.concatenate([txt_v, img_v]), jnp.concatenate([txt_valid, all_video]))
    img_out = (img_hidden.astype(jnp.float32) + img_gate * jnp.dot(img_attn, img_out_w, preferred_element_type=jnp.float32)).astype(jnp.bfloat16)
    txt_out = (txt_hidden.astype(jnp.float32) + txt_gate * jnp.dot(txt_attn, txt_out_w, preferred_element_type=jnp.float32)).astype(jnp.bfloat16)
    return (img_out, txt_out, fresh_kv)
```

```python
import functools
import math

import jax
import jax.numpy as jnp
from jax import lax
from jax.experimental import pallas as pl
from jax.experimental.pallas import tpu as pltpu
from jax.sharding import PartitionSpec as P

HEADS = 12
HD = 128
GROUPS = 4
PER = HEADS // GROUPS
GW = PER * HD
HW = HEADS * HD
LOC = 128
LOW = -1e30
SCALE = 1.0 / math.sqrt(HD)
LOG2E = 1.0 / math.log(2.0)
F32 = jnp.float32
BF16 = jnp.bfloat16


def nt(x, y):
    return lax.dot_general(x, y, (((1,), (1,)), ((), ())), preferred_element_type=F32)


def lanes_of(rows):
    return lax.broadcasted_iota(jnp.int32, (rows, HD), 1)


def normed(x, gain):
    x = x.astype(F32)
    return (x * lax.rsqrt(jnp.mean(x * x, axis=-1, keepdims=True) + 1e-06) * gain).astype(BF16)


def soft(scores, values):
    top = jnp.max(scores, axis=-1, keepdims=True)
    weights = jnp.exp2((scores - top) * (SCALE * LOG2E))
    total = jnp.sum(weights, axis=-1, keepdims=True)
    mixed = jnp.dot(weights.astype(BF16), values, preferred_element_type=F32)
    return mixed / total, top * SCALE + jnp.log(total)


def pack(logs, rows):
    lane = lanes_of(rows)
    out = jnp.zeros((rows, HD), F32)
    for j, log in enumerate(logs):
        high = log.astype(BF16).astype(F32)
        rest = log - high
        mid = rest.astype(BF16).astype(F32)
        for i, part in enumerate((high, mid, rest - mid)):
            out = jnp.where(lane == 3 * j + i, part, out)
    return out.astype(BF16)


def unpack(block, j, rows):
    lane = lanes_of(rows)
    stats = block[:, GW : GW + HD].astype(F32)
    return jnp.sum(
        jnp.where((lane >= 3 * j) & (lane < 3 * j + 3), stats, 0.0), axis=-1, keepdims=True
    )


def merge(parts):
    top = functools.reduce(jnp.maximum, [log for _, log in parts])
    shares = [jnp.exp(log - top) for _, log in parts]
    total = functools.reduce(jnp.add, shares)
    mixed = functools.reduce(jnp.add, [share * part for share, (part, _) in zip(shares, parts)])
    return mixed / total, top + jnp.log(total)


def kernel(
    n,
    img_hidden,
    img_qkv,
    stale,
    txt_hidden,
    txt_qkv,
    txt_mask,
    img_gain,
    txt_gain,
    img_gate,
    txt_gate,
    w_hbm,
    txt_w,
    img_out,
    txt_out,
    fresh,
    kvbuf,
    qsend,
    qrecv,
    kfull,
    vfull,
    kloc,
    vloc,
    oloc,
    lloc,
    osend,
    orecv,
    tsend,
    tz,
    tpl,
    tfin,
    wbuf,
    acc,
    w_sem,
    kv_recv,
    a2a_send,
    sib_send,
    row_send,
    q_send,
    q_recv,
    o_send,
    o_recv,
    tz_send,
    tz_recv,
    tp_send,
    tp_recv,
    tf_send,
    tf_recv,
):
    A = GROUPS
    B = n // A
    rows = img_qkv.shape[0]
    trows = txt_qkv.shape[0]
    me = lax.axis_index("patch")
    a = me // B
    b = lax.rem(me, B)
    core = lax.rem(b, 2)
    sib = b + 1 - 2 * core
    chip = b // 2
    chips = B // 2

    def over(k):
        return lax.rem(a + k, A)

    def row_peer(j):
        return 2 * lax.rem(chip + j, chips) + core

    def remote(src, dst, send, recv, to_a, to_b):
        return pltpu.make_async_remote_copy(
            src_ref=src,
            dst_ref=dst,
            send_sem=send,
            recv_sem=recv,
            device_id={"patch": to_a * B + to_b},
            device_id_type=pl.DeviceIdType.MESH,
        )

    def got(dst, sem):
        remote(dst, dst, sem, sem, a, sib).wait_recv()

    started = []

    def go(copy):
        copy.start()
        started.append(copy)

    load_w = pltpu.make_async_copy(w_hbm, wbuf, w_sem)
    load_w.start()

    barrier = pltpu.get_barrier_semaphore()
    for k in range(1, A):
        pl.semaphore_signal(
            barrier, inc=1, device_id={"patch": over(k) * B + b}, device_id_type=pl.DeviceIdType.MESH
        )
    for k in range(1, B):
        pl.semaphore_signal(
            barrier,
            inc=1,
            device_id={"patch": a * B + lax.rem(b + k, B)},
            device_id_type=pl.DeviceIdType.MESH,
        )
    pl.semaphore_wait(barrier, A + B - 2)

    def cols(group):
        return pl.ds(pl.multiple_of(group * GW, GW), GW)

    def slot(bb, aa):
        return bb * A + aa

    mine = slot(b, a)
    for k in range(1, A):
        go(
            remote(
                stale.at[:, :, cols(over(k))],
                kvbuf.at[mine],
                a2a_send.at[k],
                kv_recv.at[mine],
                over(k),
                b,
            )
        )

    def spread(k):
        s = slot(b, over(k))
        for j in range(1, chips):
            go(
                remote(
                    kvbuf.at[s],
                    kvbuf.at[s],
                    row_send.at[k * chips + j],
                    kv_recv.at[s],
                    a,
                    row_peer(j),
                )
            )
        go(remote(kvbuf.at[s], kvbuf.at[s], sib_send.at[k], kv_recv.at[s], a, sib))

    def forward(k):
        for j in range(1, chips):
            s = slot(row_peer(j), over(k))
            got(kvbuf.at[s], kv_recv.at[s])
            go(remote(kvbuf.at[s], kvbuf.at[s], sib_send.at[j * A + k], kv_recv.at[s], a, sib))

    kvbuf[mine] = stale[:, :, cols(a)]
    spread(0)

    for h in range(HEADS):
        c = slice(h * HD, (h + 1) * HD)
        qsend[:, c] = normed(img_qkv[:, c], img_gain[0:1, :])
    for k in range(1, A):
        go(
            remote(
                qsend.at[:, cols(over(k))], qrecv.at[a], q_send.at[k], q_recv.at[a], over(k), b
            )
        )
    qrecv[a] = qsend[:, cols(a)]

    pad = jnp.zeros((LOC - rows - trows, HD), F32)
    for h in range(HEADS):
        c = slice(h * HD, (h + 1) * HD)
        ck = slice(HW + h * HD, HW + (h + 1) * HD)
        cv = slice(2 * HW + h * HD, 2 * HW + (h + 1) * HD)
        own = normed(img_qkv[:, ck], img_gain[1:2, :])
        fresh[0, :, c] = own
        value = img_qkv[:, cv]
        fresh[1, :, c] = value
        text = normed(txt_qkv[:, ck], txt_gain[1:2, :])
        kloc[:, c] = jnp.concatenate([own.astype(F32), text.astype(F32), pad]).astype(BF16)
        vloc[:, c] = jnp.concatenate(
            [value.astype(F32), txt_qkv[:, cv].astype(F32), pad]
        ).astype(BF16)

    lane = lax.broadcasted_iota(jnp.int32, (1, LOC), 1)
    real = txt_mask[...] == 1
    in_text = (lane >= rows) & (lane < rows + trows) & real
    bias_img = jnp.where((lane < rows) | in_text, 0.0, LOW)
    bias_txt = jnp.where((lane < rows) | (in_text & (me == 0)), 0.0, LOW)

    for g in range(GROUPS):
        logs = []
        for j in range(PER):
            h = g * PER + j
            c = slice(h * HD, (h + 1) * HD)
            query = normed(txt_qkv[:, c], txt_gain[0:1, :])
            mixed, log = soft(nt(query, kloc[:, c]) + bias_txt, vloc[:, c])
            tsend[g, :, j * HD : (j + 1) * HD] = mixed.astype(BF16)
            logs.append(log)
        tsend[g, :, GW:] = pack(logs, trows)
    for k in range(1, A):
        go(remote(tsend.at[over(k)], tz.at[a], tz_send.at[k], tz_recv.at[a], over(k), b))
    tz[a] = tsend[a]

    def local_heads(first, last):
        stats = lloc[...] if first else jnp.zeros((rows, HD), F32)
        spot = lanes_of(rows)
        for h in range(first, last):
            c = slice(h * HD, (h + 1) * HD)
            mixed, log = soft(nt(qsend[:, c], kloc[:, c]) + bias_img, vloc[:, c])
            oloc[:, c] = mixed
            stats = jnp.where(spot == h, log, stats)
        lloc[...] = stats

    def assemble(bb):
        for i in range(A // 2):
            s = slot(bb, 2 * i)
            at = pl.ds(pl.multiple_of(s * rows, 2 * rows), 2 * rows)
            for which, full in ((0, kfull), (1, vfull)):
                full[at, :] = jnp.concatenate(
                    [kvbuf[s, which].astype(F32), kvbuf[s + 1, which].astype(F32)]
                ).astype(BF16)

    step = HEADS // (A - 1)
    for k in range(1, A):
        s = slot(b, over(k))
        got(kvbuf.at[s], kv_recv.at[s])
        spread(k)
        forward(k - 1)
        local_heads((k - 1) * step, k * step)

    def merge_text(blocks, where):
        logs = []
        for j in range(PER):
            c = slice(j * HD, (j + 1) * HD)
            mixed, log = merge(
                [(blk[:, c].astype(F32), unpack(blk, j, trows)) for blk in blocks]
            )
            where(c, mixed.astype(BF16))
            logs.append(log)
        return logs

    for k in range(1, A):
        got(tz.at[over(k)], tz_recv.at[over(k)])

    def put_plane(c, mixed):
        tpl[b, :, c] = mixed

    tpl[b, :, GW:] = pack(merge_text([tz[i] for i in range(A)], put_plane), trows)
    for k in range(1, B):
        go(remote(tpl.at[b], tpl.at[b], tp_send.at[k], tp_recv.at[b], a, lax.rem(b + k, B)))

    assemble(b)
    forward(A - 1)
    for j in range(1, chips):
        assemble(row_peer(j))

    for k in range(1, B):
        other = lax.rem(b + k, B)
        got(tpl.at[other], tp_recv.at[other])

    def put_final(c, mixed):
        tfin[a, :, c] = mixed

    merge_text([tpl[i] for i in range(B)], put_final)
    for k in range(1, A):
        go(remote(tfin.at[a], tfin.at[a], tf_send.at[k], tf_recv.at[a], over(k), b))

    for j in range(chips):
        bb = 2 * lax.rem(chip + j, chips) + 1 - core
        for k in range(A):
            s = slot(bb, over(k))
            got(kvbuf.at[s], kv_recv.at[s])
        assemble(bb)
    for k in range(1, A):
        got(qrecv.at[over(k)], q_recv.at[over(k)])

    place = lax.broadcasted_iota(jnp.int32, (1, n * rows), 1)

    def attend(group, out):
        start = slot(b, group) * rows
        bias = jnp.where((place >= start) & (place < start + rows), LOW, 0.0)
        logs = []
        for j in range(PER):
            c = slice(j * HD, (j + 1) * HD)
            mixed, log = soft(nt(qrecv[group, :, c], kfull[:, c]) + bias, vfull[:, c])
            out[:, c] = mixed.astype(BF16)
            logs.append(log)
        out[:, GW:] = pack(logs, rows)

    for k in range(1, A):
        attend(over(k), osend.at[k])
        go(remote(osend.at[k], orecv.at[a], o_send.at[k], o_recv.at[a], over(k), b))
    attend(a, orecv.at[a])

    for k in range(1, A):
        got(tfin.at[over(k)], tf_recv.at[over(k)])
    text = jnp.concatenate([tfin[i] for i in range(A)], axis=1)
    txt_out[...] = (
        txt_hidden[...].astype(F32)
        + txt_gate[...] * jnp.dot(text, txt_w[...], preferred_element_type=F32)
    ).astype(BF16)

    load_w.wait()
    width = img_hidden.shape[1]
    tile = width // 4
    spot = lanes_of(rows)
    for k in range(A):
        group = over(A - k) if k else a
        if k:
            got(orecv.at[group], o_recv.at[group])
        block = orecv[group]
        base = oloc[:, cols(group)]
        attn = []
        for j in range(PER):
            c = slice(j * HD, (j + 1) * HD)
            log = jnp.sum(
                jnp.where(spot == group * PER + j, lloc[...], 0.0), axis=-1, keepdims=True
            )
            mixed, _ = merge(
                [(block[:, c].astype(F32), unpack(block, j, rows)), (base[:, c], log)]
            )
            attn.append(mixed.astype(BF16))
        attn = jnp.concatenate(attn, axis=1)
        for t in range(4):
            c = slice(t * tile, (t + 1) * tile)
            part = jnp.dot(attn, wbuf[cols(group), c], preferred_element_type=F32)
            if k:
                part = acc[:, c] + part
            if k < A - 1:
                acc[:, c] = part
            else:
                img_out[:, c] = (
                    img_hidden[:, c].astype(F32) + img_gate[:, c] * part
                ).astype(BF16)

    for copy in started:
        copy.wait_send()


def body(
    img_hidden,
    img_qkv,
    stale_kv,
    txt_hidden,
    txt_qkv,
    txt_mask,
    img_qk_gain,
    txt_qk_gain,
    img_gate,
    txt_gate,
    img_out_w,
    txt_out_w,
):
    n = lax.axis_size("patch")
    A = GROUPS
    B = n // A
    rows, width = img_hidden.shape
    trows = txt_qkv.shape[0]
    mask = jnp.pad(txt_mask, (rows, LOC - rows - trows)).reshape(1, LOC)
    vmem = pl.BlockSpec(memory_space=pltpu.VMEM)
    dma = pltpu.SemaphoreType.DMA
    return pl.pallas_call(
        functools.partial(kernel, n),
        out_shape=(
            jax.ShapeDtypeStruct(img_hidden.shape, BF16),
            jax.ShapeDtypeStruct(txt_hidden.shape, BF16),
            jax.ShapeDtypeStruct(stale_kv.shape, BF16),
        ),
        in_specs=[vmem] * 10 + [pl.BlockSpec(memory_space=pl.ANY), vmem],
        out_specs=(vmem, vmem, vmem),
        scratch_shapes=[
            pltpu.VMEM((n, 2, rows, GW), BF16),
            pltpu.VMEM((rows, HW), BF16),
            pltpu.VMEM((A, rows, GW), BF16),
            pltpu.VMEM((n * rows, GW), BF16),
            pltpu.VMEM((n * rows, GW), BF16),
            pltpu.VMEM((LOC, HW), BF16),
            pltpu.VMEM((LOC, HW), BF16),
            pltpu.VMEM((rows, HW), F32),
            pltpu.VMEM((rows, HD), F32),
            pltpu.VMEM((A, rows, GW + HD), BF16),
            pltpu.VMEM((A, rows, GW + HD), BF16),
            pltpu.VMEM((A, trows, GW + HD), BF16),
            pltpu.VMEM((A, trows, GW + HD), BF16),
            pltpu.VMEM((B, trows, GW + HD), BF16),
            pltpu.VMEM((A, trows, GW), BF16),
            pltpu.VMEM(img_out_w.shape, BF16),
            pltpu.VMEM((rows, width), F32),
            dma,
            dma((n,)),
            dma((A,)),
            dma((n,)),
            dma((n,)),
            dma((A,)),
            dma((A,)),
            dma((A,)),
            dma((A,)),
            dma((A,)),
            dma((A,)),
            dma((B,)),
            dma((B,)),
            dma((A,)),
            dma((A,)),
        ],
        compiler_params=pltpu.CompilerParams(
            collective_id=0, has_side_effects=True, vmem_limit_bytes=48 * 1024 * 1024
        ),
        name="joint_attention",
    )(
        img_hidden,
        img_qkv,
        stale_kv,
        txt_hidden,
        txt_qkv,
        mask,
        img_qk_gain,
        txt_qk_gain,
        img_gate.reshape(1, -1),
        txt_gate.reshape(1, -1),
        img_out_w,
        txt_out_w,
    )


def solution(mesh):
    placed = (
        P(("group", "patch"), None),
        P(("group", "patch"), None),
        P(None, ("group", "patch"), None),
        P("group", "patch"),
        P("group", None),
        P("group"),
        P(),
        P(),
        P("group"),
        P(("group", "patch")),
        P(),
        P(None, "patch"),
    )
    return jax.shard_map(
        body,
        mesh=mesh,
        in_specs=placed,
        out_specs=(
            P(("group", "patch"), None),
            P("group", "patch"),
            P(None, ("group", "patch"), None),
        ),
        check_vma=False,
    )
```

```python
import functools
import math

import jax
import jax.numpy as jnp
from jax import lax
from jax.experimental import pallas as pl
from jax.experimental.pallas import tpu as pltpu
from jax.sharding import PartitionSpec as P

HEADS = 12
HD = 128
GROUPS = 4
PER = HEADS // GROUPS
GW = PER * HD
HW = HEADS * HD
LOC = 128
LOW = -1e30
SCALE = 1.0 / math.sqrt(HD)
LOG2E = 1.0 / math.log(2.0)
F32 = jnp.float32
BF16 = jnp.bfloat16


def nt(x, y):
    return lax.dot_general(x, y, (((1,), (1,)), ((), ())), preferred_element_type=F32)


def lanes_of(rows):
    return lax.broadcasted_iota(jnp.int32, (rows, HD), 1)


def normed(x, gain):
    x = x.astype(F32)
    return (x * lax.rsqrt(jnp.mean(x * x, axis=-1, keepdims=True) + 1e-06) * gain).astype(BF16)


def soft(scores, values):
    top = jnp.max(scores, axis=-1, keepdims=True)
    weights = jnp.exp2((scores - top) * (SCALE * LOG2E))
    total = jnp.sum(weights, axis=-1, keepdims=True)
    mixed = jnp.dot(weights.astype(BF16), values, preferred_element_type=F32)
    return mixed / total, top * SCALE + jnp.log(total)


def pack(logs, rows):
    lane = lanes_of(rows)
    out = jnp.zeros((rows, HD), F32)
    for j, log in enumerate(logs):
        high = log.astype(BF16).astype(F32)
        rest = log - high
        mid = rest.astype(BF16).astype(F32)
        for i, part in enumerate((high, mid, rest - mid)):
            out = jnp.where(lane == 3 * j + i, part, out)
    return out.astype(BF16)


def unpack(block, j, rows):
    lane = lanes_of(rows)
    stats = block[:, GW : GW + HD].astype(F32)
    return jnp.sum(
        jnp.where((lane >= 3 * j) & (lane < 3 * j + 3), stats, 0.0), axis=-1, keepdims=True
    )


def merge(parts):
    top = functools.reduce(jnp.maximum, [log for _, log in parts])
    shares = [jnp.exp(log - top) for _, log in parts]
    total = functools.reduce(jnp.add, shares)
    mixed = functools.reduce(jnp.add, [share * part for share, (part, _) in zip(shares, parts)])
    return mixed / total, top + jnp.log(total)


def kernel(
    n,
    img_hidden_hbm,
    img_qkv_hbm,
    stale,
    txt_hidden_hbm,
    txt_qkv_hbm,
    txt_mask_hbm,
    img_gain_hbm,
    txt_gain_hbm,
    img_gate_hbm,
    txt_gate_hbm,
    w_hbm,
    txt_w_hbm,
    img_out,
    txt_out,
    fresh_hbm,
    img_hidden,
    img_qkv,
    txt_hidden,
    txt_qkv,
    txt_mask,
    img_gain,
    txt_gain,
    img_gate,
    txt_gate,
    txt_w,
    wide_mask,
    fresh,
    kvbuf,
    qsend,
    qrecv,
    kfull,
    vfull,
    kloc,
    vloc,
    oloc,
    lloc,
    osend,
    orecv,
    tsend,
    tz,
    tpl,
    tfin,
    wbuf,
    acc,
    load_sem,
    fresh_sem,
    own_sem,
    kv_recv,
    a2a_send,
    sib_send,
    row_send,
    q_send,
    q_recv,
    o_send,
    o_recv,
    tz_send,
    tz_recv,
    tp_send,
    tp_recv,
    tf_send,
    tf_recv,
):
    A = GROUPS
    B = n // A
    rows = img_qkv.shape[0]
    trows = txt_qkv.shape[0]
    me = lax.axis_index("patch")
    a = me // B
    b = lax.rem(me, B)
    core = lax.rem(b, 2)
    sib = b + 1 - 2 * core
    chip = b // 2
    chips = B // 2

    def over(k):
        return lax.rem(a + k, A)

    def row_peer(j):
        return 2 * lax.rem(chip + j, chips) + core

    def remote(src, dst, send, recv, to_a, to_b):
        return pltpu.make_async_remote_copy(
            src_ref=src,
            dst_ref=dst,
            send_sem=send,
            recv_sem=recv,
            device_id={"patch": to_a * B + to_b},
            device_id_type=pl.DeviceIdType.MESH,
        )

    def got(dst, sem):
        remote(dst, dst, sem, sem, a, sib).wait_recv()

    started = []

    def go(copy):
        copy.start()
        started.append(copy)

    loads = [
        pltpu.make_async_copy(src, dst, load_sem.at[i])
        for i, (src, dst) in enumerate(
            (
                (img_qkv_hbm, img_qkv),
                (img_gain_hbm, img_gain),
                (txt_qkv_hbm, txt_qkv),
                (txt_gain_hbm, txt_gain),
                (txt_mask_hbm, txt_mask),
                (txt_w_hbm, txt_w),
                (txt_hidden_hbm, txt_hidden),
                (txt_gate_hbm, txt_gate),
                (img_hidden_hbm, img_hidden),
                (img_gate_hbm, img_gate),
                (w_hbm, wbuf),
            )
        )
    ]
    for load in loads[:5]:
        load.start()

    barrier = pltpu.get_barrier_semaphore()
    for k in range(1, A):
        pl.semaphore_signal(
            barrier, inc=1, device_id={"patch": over(k) * B + b}, device_id_type=pl.DeviceIdType.MESH
        )
    for k in range(1, B):
        pl.semaphore_signal(
            barrier,
            inc=1,
            device_id={"patch": a * B + lax.rem(b + k, B)},
            device_id_type=pl.DeviceIdType.MESH,
        )
    def cols(group):
        return pl.ds(pl.multiple_of(group * GW, GW), GW)

    def slot(bb, aa):
        return bb * A + aa

    mine = slot(b, a)
    own_copy = pltpu.make_async_copy(stale.at[:, :, cols(a)], kvbuf.at[mine], own_sem)
    own_copy.start()
    pl.semaphore_wait(barrier, A + B - 2)
    for k in range(1, A):
        go(
            remote(
                stale.at[:, :, cols(over(k))],
                kvbuf.at[mine],
                a2a_send.at[k],
                kv_recv.at[mine],
                over(k),
                b,
            )
        )

    def spread(k):
        s = slot(b, over(k))
        for j in range(1, chips):
            go(
                remote(
                    kvbuf.at[s],
                    kvbuf.at[s],
                    row_send.at[k * chips + j],
                    kv_recv.at[s],
                    a,
                    row_peer(j),
                )
            )
        go(remote(kvbuf.at[s], kvbuf.at[s], sib_send.at[k], kv_recv.at[s], a, sib))

    def forward(k):
        for j in range(1, chips):
            s = slot(row_peer(j), over(k))
            got(kvbuf.at[s], kv_recv.at[s])
            go(remote(kvbuf.at[s], kvbuf.at[s], sib_send.at[j * A + k], kv_recv.at[s], a, sib))

    own_copy.wait()
    spread(0)
    for load in loads[5:]:
        load.start()
    for load in loads[:2]:
        load.wait()

    for h in range(HEADS):
        c = slice(h * HD, (h + 1) * HD)
        qsend[:, c] = normed(img_qkv[:, c], img_gain[0:1, :])
    for k in range(1, A):
        go(
            remote(
                qsend.at[:, cols(over(k))], qrecv.at[a], q_send.at[k], q_recv.at[a], over(k), b
            )
        )
    qrecv[a] = qsend[:, cols(a)]

    for load in loads[2:5]:
        load.wait()
    pad = jnp.zeros((LOC - rows - trows, HD), F32)
    for h in range(HEADS):
        c = slice(h * HD, (h + 1) * HD)
        ck = slice(HW + h * HD, HW + (h + 1) * HD)
        cv = slice(2 * HW + h * HD, 2 * HW + (h + 1) * HD)
        own = normed(img_qkv[:, ck], img_gain[1:2, :])
        fresh[0, :, c] = own
        value = img_qkv[:, cv]
        fresh[1, :, c] = value
        text = normed(txt_qkv[:, ck], txt_gain[1:2, :])
        kloc[:, c] = jnp.concatenate([text.astype(F32), own.astype(F32), pad]).astype(BF16)
        vloc[:, c] = jnp.concatenate(
            [txt_qkv[:, cv].astype(F32), value.astype(F32), pad]
        ).astype(BF16)

    keep_fresh = pltpu.make_async_copy(fresh, fresh_hbm, fresh_sem)
    keep_fresh.start()

    lane = lax.broadcasted_iota(jnp.int32, (1, LOC), 1)
    wide_mask[...] = jnp.zeros((1, LOC), jnp.int32)
    wide_mask[:, :trows] = txt_mask[...]
    in_text = wide_mask[...] == 1
    in_img = (lane >= trows) & (lane < trows + rows)
    bias_img = jnp.where(in_img | in_text, 0.0, LOW)
    bias_txt = jnp.where(in_img | (in_text & (me == 0)), 0.0, LOW)

    for g in range(GROUPS):
        logs = []
        for j in range(PER):
            h = g * PER + j
            c = slice(h * HD, (h + 1) * HD)
            query = normed(txt_qkv[:, c], txt_gain[0:1, :])
            mixed, log = soft(nt(query, kloc[:, c]) + bias_txt, vloc[:, c])
            tsend[g, :, j * HD : (j + 1) * HD] = mixed.astype(BF16)
            logs.append(log)
        tsend[g, :, GW:] = pack(logs, trows)
    for k in range(1, A):
        go(remote(tsend.at[over(k)], tz.at[a], tz_send.at[k], tz_recv.at[a], over(k), b))
    tz[a] = tsend[a]

    def local_heads(first, last):
        stats = lloc[...] if first else jnp.zeros((rows, HD), F32)
        spot = lanes_of(rows)
        for h in range(first, last):
            c = slice(h * HD, (h + 1) * HD)
            mixed, log = soft(nt(qsend[:, c], kloc[:, c]) + bias_img, vloc[:, c])
            oloc[:, c] = mixed
            stats = jnp.where(spot == h, log, stats)
        lloc[...] = stats

    def assemble(bb):
        for i in range(A // 2):
            s = slot(bb, 2 * i)
            at = pl.ds(pl.multiple_of(s * rows, 2 * rows), 2 * rows)
            for which, full in ((0, kfull), (1, vfull)):
                full[at, :] = jnp.concatenate(
                    [kvbuf[s, which].astype(F32), kvbuf[s + 1, which].astype(F32)]
                ).astype(BF16)

    step = HEADS // (A - 1)
    for k in range(1, A):
        s = slot(b, over(k))
        got(kvbuf.at[s], kv_recv.at[s])
        spread(k)
        forward(k - 1)
        local_heads((k - 1) * step, k * step)

    def merge_text(blocks, where):
        logs = []
        for j in range(PER):
            c = slice(j * HD, (j + 1) * HD)
            mixed, log = merge(
                [(blk[:, c].astype(F32), unpack(blk, j, trows)) for blk in blocks]
            )
            where(c, mixed.astype(BF16))
            logs.append(log)
        return logs

    for k in range(1, A):
        got(tz.at[over(k)], tz_recv.at[over(k)])

    def put_plane(c, mixed):
        tpl[b, :, c] = mixed

    tpl[b, :, GW:] = pack(merge_text([tz[i] for i in range(A)], put_plane), trows)
    for k in range(1, B):
        go(remote(tpl.at[b], tpl.at[b], tp_send.at[k], tp_recv.at[b], a, lax.rem(b + k, B)))

    assemble(b)
    forward(A - 1)
    for j in range(1, chips):
        assemble(row_peer(j))

    for k in range(1, B):
        other = lax.rem(b + k, B)
        got(tpl.at[other], tp_recv.at[other])

    def put_final(c, mixed):
        tfin[a, :, c] = mixed

    merge_text([tpl[i] for i in range(B)], put_final)
    for k in range(1, A):
        go(remote(tfin.at[a], tfin.at[a], tf_send.at[k], tf_recv.at[a], over(k), b))

    for j in range(chips):
        bb = 2 * lax.rem(chip + j, chips) + 1 - core
        for k in range(A):
            s = slot(bb, over(k))
            got(kvbuf.at[s], kv_recv.at[s])
        assemble(bb)
    for k in range(1, A):
        got(qrecv.at[over(k)], q_recv.at[over(k)])

    place = lax.broadcasted_iota(jnp.int32, (1, n * rows), 1)

    def attend(group, out):
        start = slot(b, group) * rows
        bias = jnp.where((place >= start) & (place < start + rows), LOW, 0.0)
        logs = []
        for j in range(PER):
            c = slice(j * HD, (j + 1) * HD)
            mixed, log = soft(nt(qrecv[group, :, c], kfull[:, c]) + bias, vfull[:, c])
            out[:, c] = mixed.astype(BF16)
            logs.append(log)
        out[:, GW:] = pack(logs, rows)

    for k in range(1, A):
        attend(over(k), osend.at[k])
        go(remote(osend.at[k], orecv.at[a], o_send.at[k], o_recv.at[a], over(k), b))
    attend(a, orecv.at[a])

    for k in range(1, A):
        got(tfin.at[over(k)], tf_recv.at[over(k)])
    for load in loads[5:]:
        load.wait()
    text = jnp.concatenate([tfin[i] for i in range(A)], axis=1)
    txt_out[...] = (
        txt_hidden[...].astype(F32)
        + txt_gate[...] * nt(text, txt_w[...])
    ).astype(BF16)

    width = img_hidden.shape[1]
    tile = width // 4
    spot = lanes_of(rows)
    for k in range(A):
        group = over(A - k) if k else a
        if k:
            got(orecv.at[group], o_recv.at[group])
        block = orecv[group]
        base = oloc[:, cols(group)]
        attn = []
        for j in range(PER):
            c = slice(j * HD, (j + 1) * HD)
            log = jnp.sum(
                jnp.where(spot == group * PER + j, lloc[...], 0.0), axis=-1, keepdims=True
            )
            mixed, _ = merge(
                [(block[:, c].astype(F32), unpack(block, j, rows)), (base[:, c], log)]
            )
            attn.append(mixed.astype(BF16))
        attn = jnp.concatenate(attn, axis=1)
        for t in range(4):
            c = slice(t * tile, (t + 1) * tile)
            part = jnp.dot(attn, wbuf[cols(group), c], preferred_element_type=F32)
            if k:
                part = acc[:, c] + part
            if k < A - 1:
                acc[:, c] = part
            else:
                img_out[:, c] = (
                    img_hidden[:, c].astype(F32) + img_gate[:, c] * part
                ).astype(BF16)

    keep_fresh.wait()
    for copy in started:
        copy.wait_send()


def body(
    img_hidden,
    img_qkv,
    stale_kv,
    txt_hidden,
    txt_qkv,
    txt_mask,
    img_qk_gain,
    txt_qk_gain,
    img_gate,
    txt_gate,
    img_out_w,
    txt_out_w,
):
    n = lax.axis_size("patch")
    A = GROUPS
    B = n // A
    rows, width = img_hidden.shape
    trows = txt_qkv.shape[0]
    vmem = pl.BlockSpec(memory_space=pltpu.VMEM)
    dma = pltpu.SemaphoreType.DMA
    return pl.pallas_call(
        functools.partial(kernel, n),
        out_shape=(
            jax.ShapeDtypeStruct(img_hidden.shape, BF16),
            jax.ShapeDtypeStruct(txt_hidden.shape, BF16),
            jax.ShapeDtypeStruct(stale_kv.shape, BF16),
        ),
        in_specs=[pl.BlockSpec(memory_space=pltpu.HBM)] * 12,
        out_specs=(vmem, vmem, pl.BlockSpec(memory_space=pltpu.HBM)),
        scratch_shapes=[
            pltpu.VMEM(img_hidden.shape, BF16),
            pltpu.VMEM(img_qkv.shape, BF16),
            pltpu.VMEM(txt_hidden.shape, BF16),
            pltpu.VMEM(txt_qkv.shape, BF16),
            pltpu.VMEM((1, trows), jnp.int32),
            pltpu.VMEM(img_qk_gain.shape, F32),
            pltpu.VMEM(txt_qk_gain.shape, F32),
            pltpu.VMEM((1, width), F32),
            pltpu.VMEM((1, txt_gate.shape[0]), F32),
            pltpu.VMEM(txt_out_w.shape[::-1], BF16),
            pltpu.VMEM((1, LOC), jnp.int32),
            pltpu.VMEM(stale_kv.shape, BF16),
            pltpu.VMEM((n, 2, rows, GW), BF16),
            pltpu.VMEM((rows, HW), BF16),
            pltpu.VMEM((A, rows, GW), BF16),
            pltpu.VMEM((n * rows, GW), BF16),
            pltpu.VMEM((n * rows, GW), BF16),
            pltpu.VMEM((LOC, HW), BF16),
            pltpu.VMEM((LOC, HW), BF16),
            pltpu.VMEM((rows, HW), F32),
            pltpu.VMEM((rows, HD), F32),
            pltpu.VMEM((A, rows, GW + HD), BF16),
            pltpu.VMEM((A, rows, GW + HD), BF16),
            pltpu.VMEM((A, trows, GW + HD), BF16),
            pltpu.VMEM((A, trows, GW + HD), BF16),
            pltpu.VMEM((B, trows, GW + HD), BF16),
            pltpu.VMEM((A, trows, GW), BF16),
            pltpu.VMEM(img_out_w.shape, BF16),
            pltpu.VMEM((rows, width), F32),
            dma((11,)),
            dma,
            dma,
            dma((n,)),
            dma((A,)),
            dma((n,)),
            dma((n,)),
            dma((A,)),
            dma((A,)),
            dma((A,)),
            dma((A,)),
            dma((A,)),
            dma((A,)),
            dma((B,)),
            dma((B,)),
            dma((A,)),
            dma((A,)),
        ],
        compiler_params=pltpu.CompilerParams(
            collective_id=0, has_side_effects=True, vmem_limit_bytes=64 * 1024 * 1024
        ),
        name="joint_attention",
    )(
        img_hidden,
        img_qkv,
        stale_kv,
        txt_hidden,
        txt_qkv,
        txt_mask.reshape(1, -1),
        img_qk_gain,
        txt_qk_gain,
        img_gate.reshape(1, -1),
        txt_gate.reshape(1, -1),
        img_out_w,
        txt_out_w.T,
    )


def solution(mesh):
    placed = (
        P(("group", "patch"), None),
        P(("group", "patch"), None),
        P(None, ("group", "patch"), None),
        P("group", "patch"),
        P("group", None),
        P("group"),
        P(),
        P(),
        P("group"),
        P(("group", "patch")),
        P(),
        P(None, "patch"),
    )
    return jax.shard_map(
        body,
        mesh=mesh,
        in_specs=placed,
        out_specs=(
            P(("group", "patch"), None),
            P("group", "patch"),
            P(None, ("group", "patch"), None),
        ),
        check_vma=False,
    )
```

```python
import functools
import math

import jax
import jax.numpy as jnp
from jax import lax
from jax.experimental import pallas as pl
from jax.experimental.pallas import tpu as pltpu
from jax.sharding import PartitionSpec as P

HEADS = 12
HD = 128
GROUPS = 4
PER = HEADS // GROUPS
GW = PER * HD
HW = HEADS * HD
LOC = 128
LOW = -1e30
SCALE = 1.0 / math.sqrt(HD)
LOG2E = 1.0 / math.log(2.0)
F32 = jnp.float32
BF16 = jnp.bfloat16


def nt(x, y):
    return lax.dot_general(x, y, (((1,), (1,)), ((), ())), preferred_element_type=F32)


def lanes_of(rows):
    return lax.broadcasted_iota(jnp.int32, (rows, HD), 1)


def normed(x, gain):
    x = x.astype(F32)
    return (x * lax.rsqrt(jnp.mean(x * x, axis=-1, keepdims=True) + 1e-06) * gain).astype(BF16)


def soft(scores, values):
    top = jnp.max(scores, axis=-1, keepdims=True)
    weights = jnp.exp2((scores - top) * (SCALE * LOG2E))
    total = jnp.sum(weights, axis=-1, keepdims=True)
    mixed = jnp.dot(weights.astype(BF16), values, preferred_element_type=F32)
    return mixed / total, top * SCALE + jnp.log(total)


def pack(logs, rows):
    lane = lanes_of(rows)
    out = jnp.zeros((rows, HD), F32)
    for j, log in enumerate(logs):
        high = log.astype(BF16).astype(F32)
        rest = log - high
        mid = rest.astype(BF16).astype(F32)
        for i, part in enumerate((high, mid, rest - mid)):
            out = jnp.where(lane == 3 * j + i, part, out)
    return out.astype(BF16)


def unpack(block, j, rows):
    lane = lanes_of(rows)
    stats = block[:, GW : GW + HD].astype(F32)
    return jnp.sum(
        jnp.where((lane >= 3 * j) & (lane < 3 * j + 3), stats, 0.0), axis=-1, keepdims=True
    )


def merge(parts):
    top = functools.reduce(jnp.maximum, [log for _, log in parts])
    shares = [jnp.exp(log - top) for _, log in parts]
    total = functools.reduce(jnp.add, shares)
    mixed = functools.reduce(jnp.add, [share * part for share, (part, _) in zip(shares, parts)])
    return mixed / total, top + jnp.log(total)


def kernel(
    n,
    img_hidden_hbm,
    img_qkv_hbm,
    stale,
    txt_hidden_hbm,
    txt_qkv_hbm,
    txt_mask_hbm,
    img_gain_hbm,
    txt_gain_hbm,
    img_gate_hbm,
    txt_gate_hbm,
    w_hbm,
    txt_w_hbm,
    img_out,
    txt_out,
    fresh_hbm,
    img_hidden,
    img_qkv,
    txt_hidden,
    txt_qkv,
    txt_mask,
    img_gain,
    txt_gain,
    img_gate,
    txt_gate,
    txt_w,
    wide_mask,
    fresh,
    kvbuf,
    qsend,
    qrecv,
    kfull,
    vfull,
    kloc,
    vloc,
    oloc,
    lloc,
    osend,
    orecv,
    tsend,
    tz,
    tpl,
    tfin,
    wbuf,
    acc,
    load_sem,
    fresh_sem,
    own_sem,
    kv_recv,
    a2a_send,
    sib_send,
    row_send,
    q_send,
    q_recv,
    o_send,
    o_recv,
    tz_send,
    tz_recv,
    tp_send,
    tp_recv,
    tf_send,
    tf_recv,
):
    A = GROUPS
    B = n // A
    rows = img_qkv.shape[0]
    trows = txt_qkv.shape[0]
    me = lax.axis_index("patch")
    a = me // B
    b = lax.rem(me, B)
    core = lax.rem(b, 2)
    sib = b + 1 - 2 * core
    chip = b // 2
    chips = B // 2

    def over(k):
        return lax.rem(a + k, A)

    def row_peer(j):
        return 2 * lax.rem(chip + j, chips) + core

    def remote(src, dst, send, recv, to_a, to_b):
        return pltpu.make_async_remote_copy(
            src_ref=src,
            dst_ref=dst,
            send_sem=send,
            recv_sem=recv,
            device_id={"patch": to_a * B + to_b},
            device_id_type=pl.DeviceIdType.MESH,
        )

    def got(dst, sem):
        remote(dst, dst, sem, sem, a, sib).wait_recv()

    started = []

    def go(copy):
        copy.start()
        started.append(copy)

    loads = [
        pltpu.make_async_copy(src, dst, load_sem.at[i])
        for i, (src, dst) in enumerate(
            (
                (img_qkv_hbm, img_qkv),
                (img_gain_hbm, img_gain),
                (txt_qkv_hbm, txt_qkv),
                (txt_gain_hbm, txt_gain),
                (txt_mask_hbm, txt_mask),
                (txt_w_hbm, txt_w),
                (txt_hidden_hbm, txt_hidden),
                (txt_gate_hbm, txt_gate),
                (img_hidden_hbm, img_hidden),
                (img_gate_hbm, img_gate),
                (w_hbm, wbuf),
            )
        )
    ]
    for load in loads[:5]:
        load.start()

    barrier = pltpu.get_barrier_semaphore()
    for k in range(1, A):
        pl.semaphore_signal(
            barrier, inc=1, device_id={"patch": over(k) * B + b}, device_id_type=pl.DeviceIdType.MESH
        )
    for k in range(1, B):
        pl.semaphore_signal(
            barrier,
            inc=1,
            device_id={"patch": a * B + lax.rem(b + k, B)},
            device_id_type=pl.DeviceIdType.MESH,
        )
    def cols(group):
        return pl.ds(pl.multiple_of(group * GW, GW), GW)

    def slot(bb, aa):
        return bb * A + aa

    mine = slot(b, a)
    own_copy = pltpu.make_async_copy(stale.at[:, :, cols(a)], kvbuf.at[mine], own_sem)
    own_copy.start()
    pl.semaphore_wait(barrier, A + B - 2)
    def exchange(which):
        for k in range(1, A):
            go(
                remote(
                    stale.at[which, :, cols(over(k))],
                    kvbuf.at[mine, which],
                    a2a_send.at[k, which],
                    kv_recv.at[mine, which],
                    over(k),
                    b,
                )
            )
        return started[-(A - 1) :]

    def left(copies):
        for copy in copies:
            copy.wait_send()
        started[:] = [copy for copy in started if all(copy is not c for c in copies)]

    def spread(k, which):
        s = slot(b, over(k))
        part = kvbuf.at[s, which]
        for j in range(1, chips):
            go(
                remote(
                    part,
                    part,
                    row_send.at[k * chips + j, which],
                    kv_recv.at[s, which],
                    a,
                    row_peer(j),
                )
            )
        go(remote(part, part, sib_send.at[k, which], kv_recv.at[s, which], a, sib))

    def forward(k, which):
        for j in range(1, chips):
            s = slot(row_peer(j), over(k))
            part = kvbuf.at[s, which]
            got(part, kv_recv.at[s, which])
            go(remote(part, part, sib_send.at[j * A + k, which], kv_recv.at[s, which], a, sib))

    keys_away = exchange(0)
    own_copy.wait()
    spread(0, 0)
    spread(0, 1)
    for load in loads[5:10]:
        load.start()
    for load in loads[:2]:
        load.wait()

    for h in range(HEADS):
        c = slice(h * HD, (h + 1) * HD)
        qsend[:, c] = normed(img_qkv[:, c], img_gain[0:1, :])
    qrecv[a] = qsend[:, cols(a)]

    left(keys_away)
    values_away = exchange(1)

    for load in loads[2:5]:
        load.wait()
    pad = jnp.zeros((LOC - rows - trows, HD), F32)
    for h in range(HEADS):
        c = slice(h * HD, (h + 1) * HD)
        ck = slice(HW + h * HD, HW + (h + 1) * HD)
        cv = slice(2 * HW + h * HD, 2 * HW + (h + 1) * HD)
        own = normed(img_qkv[:, ck], img_gain[1:2, :])
        fresh[0, :, c] = own
        value = img_qkv[:, cv]
        fresh[1, :, c] = value
        text = normed(txt_qkv[:, ck], txt_gain[1:2, :])
        kloc[:, c] = jnp.concatenate([text.astype(F32), own.astype(F32), pad]).astype(BF16)
        vloc[:, c] = jnp.concatenate(
            [txt_qkv[:, cv].astype(F32), value.astype(F32), pad]
        ).astype(BF16)

    keep_fresh = pltpu.make_async_copy(fresh, fresh_hbm, fresh_sem)
    keep_fresh.start()

    lane = lax.broadcasted_iota(jnp.int32, (1, LOC), 1)
    wide_mask[...] = jnp.zeros((1, LOC), jnp.int32)
    wide_mask[:, :trows] = txt_mask[...]
    in_text = wide_mask[...] == 1
    in_img = (lane >= trows) & (lane < trows + rows)
    bias_img = jnp.where(in_img | in_text, 0.0, LOW)
    bias_txt = jnp.where(in_img | (in_text & (me == 0)), 0.0, LOW)

    for g in range(GROUPS):
        logs = []
        for j in range(PER):
            h = g * PER + j
            c = slice(h * HD, (h + 1) * HD)
            query = normed(txt_qkv[:, c], txt_gain[0:1, :])
            mixed, log = soft(nt(query, kloc[:, c]) + bias_txt, vloc[:, c])
            tsend[g, :, j * HD : (j + 1) * HD] = mixed.astype(BF16)
            logs.append(log)
        tsend[g, :, GW:] = pack(logs, trows)
    tz[a] = tsend[a]

    def local_heads(first, last):
        stats = lloc[...] if first else jnp.zeros((rows, HD), F32)
        spot = lanes_of(rows)
        for h in range(first, last):
            c = slice(h * HD, (h + 1) * HD)
            mixed, log = soft(nt(qsend[:, c], kloc[:, c]) + bias_img, vloc[:, c])
            oloc[:, c] = mixed
            stats = jnp.where(spot == h, log, stats)
        lloc[...] = stats

    def assemble(bb):
        for i in range(A // 2):
            s = slot(bb, 2 * i)
            at = pl.ds(pl.multiple_of(s * rows, 2 * rows), 2 * rows)
            for which, full in ((0, kfull), (1, vfull)):
                full[at, :] = jnp.concatenate(
                    [kvbuf[s, which].astype(F32), kvbuf[s + 1, which].astype(F32)]
                ).astype(BF16)

    step = HEADS // (A - 1)
    forward(0, 0)
    forward(0, 1)
    for k in range(1, A):
        s = slot(b, over(k))
        got(kvbuf.at[s, 0], kv_recv.at[s, 0])
        spread(k, 0)
    left(values_away)
    for k in range(1, A):
        go(
            remote(
                qsend.at[:, cols(over(k))], qrecv.at[a], q_send.at[k], q_recv.at[a], over(k), b
            )
        )
    queries_away = started[-(A - 1) :]
    for k in range(1, A):
        s = slot(b, over(k))
        got(kvbuf.at[s, 1], kv_recv.at[s, 1])
        spread(k, 1)
    left(queries_away)
    for k in range(1, A):
        go(remote(tsend.at[over(k)], tz.at[a], tz_send.at[k], tz_recv.at[a], over(k), b))
    loads[10].start()
    for k in range(1, A):
        forward(k, 0)
        local_heads((k - 1) * step, k * step)
    for k in range(1, A):
        forward(k, 1)

    def merge_text(blocks, where):
        logs = []
        for j in range(PER):
            c = slice(j * HD, (j + 1) * HD)
            mixed, log = merge(
                [(blk[:, c].astype(F32), unpack(blk, j, trows)) for blk in blocks]
            )
            where(c, mixed.astype(BF16))
            logs.append(log)
        return logs

    for j in range(chips):
        assemble(row_peer(j) if j else b)

    for k in range(1, A):
        got(tz.at[over(k)], tz_recv.at[over(k)])

    def put_plane(c, mixed):
        tpl[b, :, c] = mixed

    tpl[b, :, GW:] = pack(merge_text([tz[i] for i in range(A)], put_plane), trows)
    for k in range(1, B):
        go(remote(tpl.at[b], tpl.at[b], tp_send.at[k], tp_recv.at[b], a, lax.rem(b + k, B)))

    for j in range(chips):
        bb = 2 * lax.rem(chip + j, chips) + 1 - core
        for k in range(A):
            s = slot(bb, over(k))
            got(kvbuf.at[s, 0], kv_recv.at[s, 0])
            got(kvbuf.at[s, 1], kv_recv.at[s, 1])
        assemble(bb)
    for k in range(1, A):
        got(qrecv.at[over(k)], q_recv.at[over(k)])

    place = lax.broadcasted_iota(jnp.int32, (1, n * rows), 1)

    def attend(group, out):
        start = slot(b, group) * rows
        bias = jnp.where((place >= start) & (place < start + rows), LOW, 0.0)
        logs = []
        for j in range(PER):
            c = slice(j * HD, (j + 1) * HD)
            mixed, log = soft(nt(qrecv[group, :, c], kfull[:, c]) + bias, vfull[:, c])
            out[:, c] = mixed.astype(BF16)
            logs.append(log)
        out[:, GW:] = pack(logs, rows)

    def put_final(c, mixed):
        tfin[a, :, c] = mixed

    for k in range(1, A):
        attend(over(k), osend.at[k])
        go(remote(osend.at[k], orecv.at[a], o_send.at[k], o_recv.at[a], over(k), b))
        if k == 1:
            for i in range(1, B):
                other = lax.rem(b + i, B)
                got(tpl.at[other], tp_recv.at[other])
            merge_text([tpl[i] for i in range(B)], put_final)
            for i in range(1, A):
                go(remote(tfin.at[a], tfin.at[a], tf_send.at[i], tf_recv.at[a], over(i), b))
    attend(a, orecv.at[a])

    for load in loads[5:]:
        load.wait()
    width = img_hidden.shape[1]
    tile = width // 4
    spot = lanes_of(rows)
    for k in range(A):
        group = over(A - k) if k else a
        if k == A - 1:
            for i in range(1, A):
                got(tfin.at[over(i)], tf_recv.at[over(i)])
            text = jnp.concatenate([tfin[i] for i in range(A)], axis=1)
            txt_out[...] = (
                txt_hidden[...].astype(F32) + txt_gate[...] * nt(text, txt_w[...])
            ).astype(BF16)
        if k:
            got(orecv.at[group], o_recv.at[group])
        block = orecv[group]
        base = oloc[:, cols(group)]
        attn = []
        for j in range(PER):
            c = slice(j * HD, (j + 1) * HD)
            log = jnp.sum(
                jnp.where(spot == group * PER + j, lloc[...], 0.0), axis=-1, keepdims=True
            )
            mixed, _ = merge(
                [(block[:, c].astype(F32), unpack(block, j, rows)), (base[:, c], log)]
            )
            attn.append(mixed.astype(BF16))
        attn = jnp.concatenate(attn, axis=1)
        for t in range(4):
            c = slice(t * tile, (t + 1) * tile)
            part = jnp.dot(attn, wbuf[cols(group), c], preferred_element_type=F32)
            if k:
                part = acc[:, c] + part
            if k < A - 1:
                acc[:, c] = part
            else:
                img_out[:, c] = (
                    img_hidden[:, c].astype(F32) + img_gate[:, c] * part
                ).astype(BF16)

    keep_fresh.wait()
    for copy in started:
        copy.wait_send()


def keep(count, *refs):
    sources, results, held = (refs[i * count : (i + 1) * count] for i in range(3))
    in_sem, out_sem = refs[3 * count :]
    loads = [
        pltpu.make_async_copy(sources[i], held[i], in_sem.at[i]) for i in range(count)
    ]
    stores = [
        pltpu.make_async_copy(held[i], results[i], out_sem.at[i]) for i in range(count)
    ]
    for load in loads:
        load.start()
    for load, store in zip(loads, stores):
        load.wait()
        store.start()
    for store in stores:
        store.wait()


def body(
    img_hidden,
    img_qkv,
    stale_kv,
    txt_hidden,
    txt_qkv,
    txt_mask,
    img_qk_gain,
    txt_qk_gain,
    img_gate,
    txt_gate,
    img_out_w,
    txt_out_w,
):
    n = lax.axis_size("patch")
    A = GROUPS
    B = n // A
    rows, width = img_hidden.shape
    trows = txt_qkv.shape[0]
    vmem = pl.BlockSpec(memory_space=pltpu.VMEM)
    dma = pltpu.SemaphoreType.DMA
    results = pl.pallas_call(
        functools.partial(kernel, n),
        out_shape=(
            jax.ShapeDtypeStruct(img_hidden.shape, BF16),
            jax.ShapeDtypeStruct(txt_hidden.shape, BF16),
            jax.ShapeDtypeStruct(stale_kv.shape, BF16),
        ),
        in_specs=[pl.BlockSpec(memory_space=pltpu.HBM)] * 12,
        out_specs=(vmem, vmem, pl.BlockSpec(memory_space=pltpu.HBM)),
        scratch_shapes=[
            pltpu.VMEM(img_hidden.shape, BF16),
            pltpu.VMEM(img_qkv.shape, BF16),
            pltpu.VMEM(txt_hidden.shape, BF16),
            pltpu.VMEM(txt_qkv.shape, BF16),
            pltpu.VMEM((1, trows), jnp.int32),
            pltpu.VMEM(img_qk_gain.shape, F32),
            pltpu.VMEM(txt_qk_gain.shape, F32),
            pltpu.VMEM((1, width), F32),
            pltpu.VMEM((1, txt_gate.shape[0]), F32),
            pltpu.VMEM(txt_out_w.shape[::-1], BF16),
            pltpu.VMEM((1, LOC), jnp.int32),
            pltpu.VMEM(stale_kv.shape, BF16),
            pltpu.VMEM((n, 2, rows, GW), BF16),
            pltpu.VMEM((rows, HW), BF16),
            pltpu.VMEM((A, rows, GW), BF16),
            pltpu.VMEM((n * rows, GW), BF16),
            pltpu.VMEM((n * rows, GW), BF16),
            pltpu.VMEM((LOC, HW), BF16),
            pltpu.VMEM((LOC, HW), BF16),
            pltpu.VMEM((rows, HW), F32),
            pltpu.VMEM((rows, HD), F32),
            pltpu.VMEM((A, rows, GW + HD), BF16),
            pltpu.VMEM((A, rows, GW + HD), BF16),
            pltpu.VMEM((A, trows, GW + HD), BF16),
            pltpu.VMEM((A, trows, GW + HD), BF16),
            pltpu.VMEM((B, trows, GW + HD), BF16),
            pltpu.VMEM((A, trows, GW), BF16),
            pltpu.VMEM(img_out_w.shape, BF16),
            pltpu.VMEM((rows, width), F32),
            dma((11,)),
            dma,
            dma,
            dma((n, 2)),
            dma((A, 2)),
            dma((n, 2)),
            dma((n, 2)),
            dma((A,)),
            dma((A,)),
            dma((A,)),
            dma((A,)),
            dma((A,)),
            dma((A,)),
            dma((B,)),
            dma((B,)),
            dma((A,)),
            dma((A,)),
        ],
        compiler_params=pltpu.CompilerParams(
            collective_id=0, has_side_effects=True, vmem_limit_bytes=64 * 1024 * 1024
        ),
        name="joint_attention",
    )(
        img_hidden,
        img_qkv,
        stale_kv,
        txt_hidden,
        txt_qkv,
        txt_mask.reshape(1, -1),
        img_qk_gain,
        txt_qk_gain,
        img_gate.reshape(1, -1),
        txt_gate.reshape(1, -1),
        img_out_w,
        txt_out_w.T,
    )
    hbm = pl.BlockSpec(memory_space=pltpu.HBM)
    return pl.pallas_call(
        functools.partial(keep, 3),
        out_shape=tuple(jax.ShapeDtypeStruct(x.shape, x.dtype) for x in results),
        in_specs=[hbm] * 3,
        out_specs=(hbm,) * 3,
        scratch_shapes=[pltpu.VMEM(x.shape, x.dtype) for x in results] + [dma((3,)), dma((3,))],
        compiler_params=pltpu.CompilerParams(vmem_limit_bytes=64 * 1024 * 1024),
        name="keep_results",
    )(*results)


def solution(mesh):
    placed = (
        P(("group", "patch"), None),
        P(("group", "patch"), None),
        P(None, ("group", "patch"), None),
        P("group", "patch"),
        P("group", None),
        P("group"),
        P(),
        P(),
        P("group"),
        P(("group", "patch")),
        P(),
        P(None, "patch"),
    )
    return jax.shard_map(
        body,
        mesh=mesh,
        in_specs=placed,
        out_specs=(
            P(("group", "patch"), None),
            P("group", "patch"),
            P(None, ("group", "patch"), None),
        ),
        check_vma=False,
    )
```

```python
import functools
import math

import jax
import jax.numpy as jnp
from jax import lax
from jax.experimental import pallas as pl
from jax.experimental.pallas import tpu as pltpu
from jax.sharding import PartitionSpec as P

HEADS = 12
HD = 128
GROUPS = 4
PER = HEADS // GROUPS
GW = PER * HD
HW = HEADS * HD
LOC = 128
STAT = 16
LOW = -1e30
SCALE = 1.0 / math.sqrt(HD)
LOG2E = 1.0 / math.log(2.0)
F32 = jnp.float32
BF16 = jnp.bfloat16


def nt(x, y):
    return lax.dot_general(x, y, (((1,), (1,)), ((), ())), preferred_element_type=F32)


def lanes_of(rows):
    return lax.broadcasted_iota(jnp.int32, (rows, HD), 1)


def normed(x, gain):
    x = x.astype(F32)
    return (x * lax.rsqrt(jnp.mean(x * x, axis=-1, keepdims=True) + 1e-06) * gain).astype(BF16)


def soft(scores, values):
    top = jnp.max(scores, axis=-1, keepdims=True)
    weights = jnp.exp2((scores - top) * (SCALE * LOG2E))
    total = jnp.sum(weights, axis=-1, keepdims=True)
    mixed = jnp.dot(weights.astype(BF16), values, preferred_element_type=F32)
    return mixed / total, top * SCALE + jnp.log(total)


def split(logs, rows):
    lane = lanes_of(rows)
    out = jnp.zeros((rows, HD), F32)
    for j, log in enumerate(logs):
        high = log.astype(BF16).astype(F32)
        rest = log - high
        mid = rest.astype(BF16).astype(F32)
        for i, part in enumerate((high, mid, rest - mid)):
            out = jnp.where(lane == 3 * j + i, part, out)
    return out


def pack(logs, rows):
    return split(logs, rows).astype(BF16)


def pack_across(logs, rows):
    full = jnp.concatenate([split(logs, rows), jnp.zeros((HD - rows, HD), F32)])
    return full.T[:STAT].astype(BF16)


def unpack_across(stats, rows):
    full = jnp.concatenate([stats.astype(F32), jnp.zeros((HD - STAT, HD), F32)])
    return full.T[:rows]


def joined(stats, j, rows):
    lane = lanes_of(rows)
    return jnp.sum(
        jnp.where((lane >= 3 * j) & (lane < 3 * j + 3), stats, 0.0), axis=-1, keepdims=True
    )


def unpack(block, j, rows):
    return joined(block[:, GW : GW + HD].astype(F32), j, rows)


def merge(parts):
    top = functools.reduce(jnp.maximum, [log for _, log in parts])
    shares = [jnp.exp(log - top) for _, log in parts]
    total = functools.reduce(jnp.add, shares)
    mixed = functools.reduce(jnp.add, [share * part for share, (part, _) in zip(shares, parts)])
    return mixed / total, top + jnp.log(total)


def kernel(
    n,
    img_hidden_hbm,
    img_qkv_hbm,
    stale,
    txt_hidden_hbm,
    txt_qkv_hbm,
    txt_mask_hbm,
    img_gain_hbm,
    txt_gain_hbm,
    img_gate_hbm,
    txt_gate_hbm,
    w_hbm,
    txt_w_hbm,
    img_out,
    txt_out,
    fresh_hbm,
    img_hidden,
    img_qkv,
    txt_hidden,
    txt_qkv,
    txt_mask,
    img_gain,
    txt_gain,
    img_gate,
    txt_gate,
    txt_w,
    wide_mask,
    fresh,
    kvbuf,
    qsend,
    qrecv,
    kfull,
    vfull,
    kloc,
    vloc,
    oloc,
    lloc,
    osend,
    orecv,
    ssend,
    srecv,
    tsend,
    tz,
    tpl,
    tfin,
    wbuf,
    acc,
    load_sem,
    fresh_sem,
    own_sem,
    kv_recv,
    a2a_send,
    sib_send,
    row_send,
    q_send,
    q_recv,
    o_send,
    o_recv,
    s_send,
    s_recv,
    tz_send,
    tz_recv,
    tp_send,
    tp_recv,
    tf_send,
    tf_recv,
):
    A = GROUPS
    B = n // A
    rows = img_qkv.shape[0]
    trows = txt_qkv.shape[0]
    me = lax.axis_index("patch")
    a = me // B
    b = lax.rem(me, B)
    core = lax.rem(b, 2)
    sib = b + 1 - 2 * core
    chip = b // 2
    chips = B // 2

    def over(k):
        return lax.rem(a + k, A)

    def row_peer(j):
        return 2 * lax.rem(chip + j, chips) + core

    def remote(src, dst, send, recv, to_a, to_b):
        return pltpu.make_async_remote_copy(
            src_ref=src,
            dst_ref=dst,
            send_sem=send,
            recv_sem=recv,
            device_id={"patch": to_a * B + to_b},
            device_id_type=pl.DeviceIdType.MESH,
        )

    def got(dst, sem):
        remote(dst, dst, sem, sem, a, sib).wait_recv()

    started = []

    def go(copy):
        copy.start()
        started.append(copy)

    loads = [
        pltpu.make_async_copy(src, dst, load_sem.at[i])
        for i, (src, dst) in enumerate(
            (
                (img_qkv_hbm, img_qkv),
                (img_gain_hbm, img_gain),
                (txt_qkv_hbm, txt_qkv),
                (txt_gain_hbm, txt_gain),
                (txt_mask_hbm, txt_mask),
                (txt_w_hbm, txt_w),
                (txt_hidden_hbm, txt_hidden),
                (txt_gate_hbm, txt_gate),
                (img_hidden_hbm, img_hidden),
                (img_gate_hbm, img_gate),
                (w_hbm, wbuf),
            )
        )
    ]
    for load in loads[:5]:
        load.start()

    barrier = pltpu.get_barrier_semaphore()
    for k in range(1, A):
        pl.semaphore_signal(
            barrier, inc=1, device_id={"patch": over(k) * B + b}, device_id_type=pl.DeviceIdType.MESH
        )
    for k in range(1, B):
        pl.semaphore_signal(
            barrier,
            inc=1,
            device_id={"patch": a * B + lax.rem(b + k, B)},
            device_id_type=pl.DeviceIdType.MESH,
        )
    def cols(group):
        return pl.ds(pl.multiple_of(group * GW, GW), GW)

    def slot(bb, aa):
        return bb * A + aa

    mine = slot(b, a)
    own_copy = pltpu.make_async_copy(stale.at[:, :, cols(a)], kvbuf.at[mine], own_sem)
    own_copy.start()
    pl.semaphore_wait(barrier, A + B - 2)
    def exchange(which):
        for k in range(1, A):
            go(
                remote(
                    stale.at[which, :, cols(over(k))],
                    kvbuf.at[mine, which],
                    a2a_send.at[k, which],
                    kv_recv.at[mine, which],
                    over(k),
                    b,
                )
            )
        return started[-(A - 1) :]

    def left(copies):
        for copy in copies:
            copy.wait_send()
        started[:] = [copy for copy in started if all(copy is not c for c in copies)]

    def spread(k, which):
        s = slot(b, over(k))
        part = kvbuf.at[s, which]
        for j in range(1, chips):
            go(
                remote(
                    part,
                    part,
                    row_send.at[k * chips + j, which],
                    kv_recv.at[s, which],
                    a,
                    row_peer(j),
                )
            )
        go(remote(part, part, sib_send.at[k, which], kv_recv.at[s, which], a, sib))

    def forward(k, which):
        for j in range(1, chips):
            s = slot(row_peer(j), over(k))
            part = kvbuf.at[s, which]
            got(part, kv_recv.at[s, which])
            go(remote(part, part, sib_send.at[j * A + k, which], kv_recv.at[s, which], a, sib))

    keys_away = exchange(0)
    own_copy.wait()
    spread(0, 0)
    spread(0, 1)
    for load in loads[5:10]:
        load.start()
    for load in loads[:2]:
        load.wait()

    for h in range(HEADS):
        c = slice(h * HD, (h + 1) * HD)
        qsend[:, c] = normed(img_qkv[:, c], img_gain[0:1, :])
    qrecv[a] = qsend[:, cols(a)]

    left(keys_away)
    values_away = exchange(1)

    for load in loads[2:5]:
        load.wait()
    pad = jnp.zeros((LOC - rows - trows, HD), F32)
    for h in range(HEADS):
        c = slice(h * HD, (h + 1) * HD)
        ck = slice(HW + h * HD, HW + (h + 1) * HD)
        cv = slice(2 * HW + h * HD, 2 * HW + (h + 1) * HD)
        own = normed(img_qkv[:, ck], img_gain[1:2, :])
        fresh[0, :, c] = own
        value = img_qkv[:, cv]
        fresh[1, :, c] = value
        text = normed(txt_qkv[:, ck], txt_gain[1:2, :])
        kloc[:, c] = jnp.concatenate([text.astype(F32), own.astype(F32), pad]).astype(BF16)
        vloc[:, c] = jnp.concatenate(
            [txt_qkv[:, cv].astype(F32), value.astype(F32), pad]
        ).astype(BF16)

    keep_fresh = pltpu.make_async_copy(fresh, fresh_hbm, fresh_sem)
    keep_fresh.start()

    lane = lax.broadcasted_iota(jnp.int32, (1, LOC), 1)
    wide_mask[...] = jnp.zeros((1, LOC), jnp.int32)
    wide_mask[:, :trows] = txt_mask[...]
    in_text = wide_mask[...] == 1
    in_img = (lane >= trows) & (lane < trows + rows)
    bias_img = jnp.where(in_img | in_text, 0.0, LOW)
    bias_txt = jnp.where(in_img | (in_text & (me == 0)), 0.0, LOW)

    for g in range(GROUPS):
        logs = []
        for j in range(PER):
            h = g * PER + j
            c = slice(h * HD, (h + 1) * HD)
            query = normed(txt_qkv[:, c], txt_gain[0:1, :])
            mixed, log = soft(nt(query, kloc[:, c]) + bias_txt, vloc[:, c])
            tsend[g, :, j * HD : (j + 1) * HD] = mixed.astype(BF16)
            logs.append(log)
        tsend[g, :, GW:] = pack(logs, trows)

    def only(condition, act):
        if B == A:
            act()
        else:
            pl.when(condition)(act)

    def beside(k):
        return lax.rem(b + k, B)

    def text_part(k):
        t = beside(k)
        return remote(tsend.at[t], tpl.at[b], tp_send.at[k], tp_recv.at[b], a, t)

    def text_group(k):
        return remote(tz.at[a], tz.at[a], tz_send.at[k], tz_recv.at[a], over(k), b)

    def text_final(k):
        return remote(tfin.at[b], tfin.at[b], tf_send.at[k], tf_recv.at[b], a, beside(k))

    for k in range(1, B):
        only(beside(k) < A, lambda k=k: text_part(k).start())

    def own_part():
        tpl[b] = tsend[b]

    only(b < A, own_part)

    def merge_text(blocks, where):
        logs = []
        for j in range(PER):
            c = slice(j * HD, (j + 1) * HD)
            mixed, log = merge(
                [(blk[:, c].astype(F32), unpack(blk, j, trows)) for blk in blocks]
            )
            where(c, mixed.astype(BF16))
            logs.append(log)
        return logs

    def over_plane():
        for k in range(1, B):
            got(tpl.at[beside(k)], tp_recv.at[beside(k)])

        def put(c, mixed):
            tz[a, :, c] = mixed

        tz[a, :, GW:] = pack(merge_text([tpl[i] for i in range(B)], put), trows)
        for k in range(1, A):
            text_group(k).start()

    def over_z():
        for k in range(1, A):
            got(tz.at[over(k)], tz_recv.at[over(k)])

        def put(c, mixed):
            tfin[b, :, c] = mixed

        merge_text([tz[i] for i in range(A)], put)
        for k in range(1, B):
            text_final(k).start()

    def local_heads(first, last):
        stats = lloc[...] if first else jnp.zeros((rows, HD), F32)
        spot = lanes_of(rows)
        for h in range(first, last):
            c = slice(h * HD, (h + 1) * HD)
            mixed, log = soft(nt(qsend[:, c], kloc[:, c]) + bias_img, vloc[:, c])
            oloc[:, c] = mixed
            stats = jnp.where(spot == h, log, stats)
        lloc[...] = stats

    def assemble(bb):
        for i in range(A // 2):
            s = slot(bb, 2 * i)
            at = pl.ds(pl.multiple_of(s * rows, 2 * rows), 2 * rows)
            for which, full in ((0, kfull), (1, vfull)):
                full[at, :] = jnp.concatenate(
                    [kvbuf[s, which].astype(F32), kvbuf[s + 1, which].astype(F32)]
                ).astype(BF16)

    step = HEADS // (A - 1)
    forward(0, 0)
    forward(0, 1)
    for k in range(1, A):
        s = slot(b, over(k))
        got(kvbuf.at[s, 0], kv_recv.at[s, 0])
        spread(k, 0)
    left(values_away)
    for k in range(1, A):
        go(
            remote(
                qsend.at[:, cols(over(k))], qrecv.at[a], q_send.at[k], q_recv.at[a], over(k), b
            )
        )
    queries_away = started[-(A - 1) :]
    for k in range(1, A):
        s = slot(b, over(k))
        got(kvbuf.at[s, 1], kv_recv.at[s, 1])
        spread(k, 1)
    left(queries_away)
    only(b < A, over_plane)
    loads[10].start()
    for k in range(1, A):
        forward(k, 0)
        local_heads((k - 1) * step, k * step)
    for k in range(1, A):
        forward(k, 1)

    for j in range(chips):
        assemble(row_peer(j) if j else b)

    for j in range(chips):
        bb = 2 * lax.rem(chip + j, chips) + 1 - core
        for k in range(A):
            s = slot(bb, over(k))
            got(kvbuf.at[s, 0], kv_recv.at[s, 0])
            got(kvbuf.at[s, 1], kv_recv.at[s, 1])
        assemble(bb)
    for k in range(1, A):
        got(qrecv.at[over(k)], q_recv.at[over(k)])

    place = lax.broadcasted_iota(jnp.int32, (1, n * rows), 1)

    def attend(group, out, stats):
        start = slot(b, group) * rows
        bias = jnp.where((place >= start) & (place < start + rows), LOW, 0.0)
        logs = []
        for j in range(PER):
            c = slice(j * HD, (j + 1) * HD)
            mixed, log = soft(nt(qrecv[group, :, c], kfull[:, c]) + bias, vfull[:, c])
            out[:, c] = mixed.astype(BF16)
            logs.append(log)
        stats[...] = pack_across(logs, rows)

    for k in range(1, A):
        attend(over(k), osend.at[k], ssend.at[k])
        go(remote(ssend.at[k], srecv.at[a], s_send.at[k], s_recv.at[a], over(k), b))
        go(remote(osend.at[k], orecv.at[a], o_send.at[k], o_recv.at[a], over(k), b))
        if k == 1:
            only(b < A, over_z)
    attend(a, orecv.at[a], srecv.at[a])

    for load in loads[5:]:
        load.wait()
    width = img_hidden.shape[1]
    tile = width // 4
    spot = lanes_of(rows)
    for k in range(A):
        group = over(A - k) if k else a
        if k == A - 1:
            for i in range(1, B):
                t = beside(i)
                only(t < A, lambda t=t: got(tfin.at[t], tf_recv.at[t]))
            text = jnp.concatenate([tfin[i] for i in range(A)], axis=1)
            txt_out[...] = (
                txt_hidden[...].astype(F32) + txt_gate[...] * nt(text, txt_w[...])
            ).astype(BF16)
        if k:
            got(orecv.at[group], o_recv.at[group])
            got(srecv.at[group], s_recv.at[group])
        block = orecv[group]
        stats = unpack_across(srecv[group], rows)
        base = oloc[:, cols(group)]
        attn = []
        for j in range(PER):
            c = slice(j * HD, (j + 1) * HD)
            log = jnp.sum(
                jnp.where(spot == group * PER + j, lloc[...], 0.0), axis=-1, keepdims=True
            )
            mixed, _ = merge(
                [(block[:, c].astype(F32), joined(stats, j, rows)), (base[:, c], log)]
            )
            attn.append(mixed.astype(BF16))
        attn = jnp.concatenate(attn, axis=1)
        for t in range(4):
            c = slice(t * tile, (t + 1) * tile)
            part = jnp.dot(attn, wbuf[cols(group), c], preferred_element_type=F32)
            if k:
                part = acc[:, c] + part
            if k < A - 1:
                acc[:, c] = part
            else:
                img_out[:, c] = (
                    img_hidden[:, c].astype(F32) + img_gate[:, c] * part
                ).astype(BF16)

    def text_left():
        for k in range(1, A):
            text_group(k).wait_send()
        for k in range(1, B):
            text_final(k).wait_send()

    for k in range(1, B):
        only(beside(k) < A, lambda k=k: text_part(k).wait_send())
    only(b < A, text_left)
    keep_fresh.wait()
    for copy in started:
        copy.wait_send()


def keep(count, *refs):
    sources, results, held = (refs[i * count : (i + 1) * count] for i in range(3))
    in_sem, out_sem = refs[3 * count :]
    loads = [
        pltpu.make_async_copy(sources[i], held[i], in_sem.at[i]) for i in range(count)
    ]
    stores = [
        pltpu.make_async_copy(held[i], results[i], out_sem.at[i]) for i in range(count)
    ]
    for load in loads:
        load.start()
    for load, store in zip(loads, stores):
        load.wait()
        store.start()
    for store in stores:
        store.wait()


def body(
    img_hidden,
    img_qkv,
    stale_kv,
    txt_hidden,
    txt_qkv,
    txt_mask,
    img_qk_gain,
    txt_qk_gain,
    img_gate,
    txt_gate,
    img_out_w,
    txt_out_w,
):
    n = lax.axis_size("patch")
    A = GROUPS
    B = n // A
    rows, width = img_hidden.shape
    trows = txt_qkv.shape[0]
    vmem = pl.BlockSpec(memory_space=pltpu.VMEM)
    dma = pltpu.SemaphoreType.DMA
    results = pl.pallas_call(
        functools.partial(kernel, n),
        out_shape=(
            jax.ShapeDtypeStruct(img_hidden.shape, BF16),
            jax.ShapeDtypeStruct(txt_hidden.shape, BF16),
            jax.ShapeDtypeStruct(stale_kv.shape, BF16),
        ),
        in_specs=[pl.BlockSpec(memory_space=pltpu.HBM)] * 12,
        out_specs=(vmem, vmem, pl.BlockSpec(memory_space=pltpu.HBM)),
        scratch_shapes=[
            pltpu.VMEM(img_hidden.shape, BF16),
            pltpu.VMEM(img_qkv.shape, BF16),
            pltpu.VMEM(txt_hidden.shape, BF16),
            pltpu.VMEM(txt_qkv.shape, BF16),
            pltpu.VMEM((1, trows), jnp.int32),
            pltpu.VMEM(img_qk_gain.shape, F32),
            pltpu.VMEM(txt_qk_gain.shape, F32),
            pltpu.VMEM((1, width), F32),
            pltpu.VMEM((1, txt_gate.shape[0]), F32),
            pltpu.VMEM(txt_out_w.shape[::-1], BF16),
            pltpu.VMEM((1, LOC), jnp.int32),
            pltpu.VMEM(stale_kv.shape, BF16),
            pltpu.VMEM((n, 2, rows, GW), BF16),
            pltpu.VMEM((rows, HW), BF16),
            pltpu.VMEM((A, rows, GW), BF16),
            pltpu.VMEM((n * rows, GW), BF16),
            pltpu.VMEM((n * rows, GW), BF16),
            pltpu.VMEM((LOC, HW), BF16),
            pltpu.VMEM((LOC, HW), BF16),
            pltpu.VMEM((rows, HW), F32),
            pltpu.VMEM((rows, HD), F32),
            pltpu.VMEM((A, rows, GW), BF16),
            pltpu.VMEM((A, rows, GW), BF16),
            pltpu.VMEM((A, STAT, HD), BF16),
            pltpu.VMEM((A, STAT, HD), BF16),
            pltpu.VMEM((A, trows, GW + HD), BF16),
            pltpu.VMEM((A, trows, GW + HD), BF16),
            pltpu.VMEM((B, trows, GW + HD), BF16),
            pltpu.VMEM((A, trows, GW), BF16),
            pltpu.VMEM(img_out_w.shape, BF16),
            pltpu.VMEM((rows, width), F32),
            dma((11,)),
            dma,
            dma,
            dma((n, 2)),
            dma((A, 2)),
            dma((n, 2)),
            dma((n, 2)),
            dma((A,)),
            dma((A,)),
            dma((A,)),
            dma((A,)),
            dma((A,)),
            dma((A,)),
            dma((A,)),
            dma((A,)),
            dma((B,)),
            dma((B,)),
            dma((B,)),
            dma((A,)),
        ],
        compiler_params=pltpu.CompilerParams(
            collective_id=0, has_side_effects=True, vmem_limit_bytes=64 * 1024 * 1024
        ),
        name="joint_attention",
    )(
        img_hidden,
        img_qkv,
        stale_kv,
        txt_hidden,
        txt_qkv,
        txt_mask.reshape(1, -1),
        img_qk_gain,
        txt_qk_gain,
        img_gate.reshape(1, -1),
        txt_gate.reshape(1, -1),
        img_out_w,
        txt_out_w.T,
    )
    hbm = pl.BlockSpec(memory_space=pltpu.HBM)
    return pl.pallas_call(
        functools.partial(keep, 3),
        out_shape=tuple(jax.ShapeDtypeStruct(x.shape, x.dtype) for x in results),
        in_specs=[hbm] * 3,
        out_specs=(hbm,) * 3,
        scratch_shapes=[pltpu.VMEM(x.shape, x.dtype) for x in results] + [dma((3,)), dma((3,))],
        compiler_params=pltpu.CompilerParams(vmem_limit_bytes=64 * 1024 * 1024),
        name="keep_results",
    )(*results)


def solution(mesh):
    placed = (
        P(("group", "patch"), None),
        P(("group", "patch"), None),
        P(None, ("group", "patch"), None),
        P("group", "patch"),
        P("group", None),
        P("group"),
        P(),
        P(),
        P("group"),
        P(("group", "patch")),
        P(),
        P(None, "patch"),
    )
    return jax.shard_map(
        body,
        mesh=mesh,
        in_specs=placed,
        out_specs=(
            P(("group", "patch"), None),
            P("group", "patch"),
            P(None, ("group", "patch"), None),
        ),
        check_vma=False,
    )
```

```python
import functools
import math

import jax
import jax.numpy as jnp
from jax import lax
from jax.experimental import pallas as pl
from jax.experimental.pallas import tpu as pltpu
from jax.sharding import PartitionSpec as P

HEADS = 12
HD = 128
GROUPS = 4
PER = HEADS // GROUPS
GW = PER * HD
HW = HEADS * HD
LOC = 128
STAT = 16
LOW = -1e30
SCALE = 1.0 / math.sqrt(HD)
LOG2E = 1.0 / math.log(2.0)
F32 = jnp.float32
BF16 = jnp.bfloat16


def nt(x, y):
    return lax.dot_general(x, y, (((1,), (1,)), ((), ())), preferred_element_type=F32)


def lanes_of(rows):
    return lax.broadcasted_iota(jnp.int32, (rows, HD), 1)


def normed(x, gain):
    x = x.astype(F32)
    return (x * lax.rsqrt(jnp.mean(x * x, axis=-1, keepdims=True) + 1e-06) * gain).astype(BF16)


def soft(scores, values):
    top = jnp.max(scores, axis=-1, keepdims=True)
    weights = jnp.exp2((scores - top) * (SCALE * LOG2E))
    total = jnp.sum(weights, axis=-1, keepdims=True)
    mixed = jnp.dot(weights.astype(BF16), values, preferred_element_type=F32)
    return mixed / total, top * SCALE + jnp.log(total)


def split(logs, rows):
    lane = lanes_of(rows)
    out = jnp.zeros((rows, HD), F32)
    for j, log in enumerate(logs):
        high = log.astype(BF16).astype(F32)
        rest = log - high
        mid = rest.astype(BF16).astype(F32)
        for i, part in enumerate((high, mid, rest - mid)):
            out = jnp.where(lane == 3 * j + i, part, out)
    return out


def pack(logs, rows):
    return split(logs, rows).astype(BF16)


def pack_across(logs, rows):
    full = jnp.concatenate([split(logs, rows), jnp.zeros((HD - rows, HD), F32)])
    return full.T[:STAT].astype(BF16)


def unpack_across(stats, rows):
    full = jnp.concatenate([stats.astype(F32), jnp.zeros((HD - STAT, HD), F32)])
    return full.T[:rows]


def joined(stats, j, rows):
    lane = lanes_of(rows)
    return jnp.sum(
        jnp.where((lane >= 3 * j) & (lane < 3 * j + 3), stats, 0.0), axis=-1, keepdims=True
    )


def unpack(block, j, rows):
    return joined(block[:, GW : GW + HD].astype(F32), j, rows)


def merge(parts):
    top = functools.reduce(jnp.maximum, [log for _, log in parts])
    shares = [jnp.exp(log - top) for _, log in parts]
    total = functools.reduce(jnp.add, shares)
    mixed = functools.reduce(jnp.add, [share * part for share, (part, _) in zip(shares, parts)])
    return mixed / total, top + jnp.log(total)


def kernel(
    n,
    img_hidden_hbm,
    img_qkv_hbm,
    stale,
    txt_hidden_hbm,
    txt_qkv_hbm,
    txt_mask_hbm,
    img_gain_hbm,
    txt_gain_hbm,
    img_gate_hbm,
    txt_gate_hbm,
    w_hbm,
    txt_w_hbm,
    img_out,
    txt_out,
    fresh_hbm,
    img_hidden,
    img_qkv,
    txt_hidden,
    txt_qkv,
    txt_mask,
    img_gain,
    txt_gain,
    img_gate,
    txt_gate,
    txt_w,
    wide_mask,
    fresh,
    kvbuf,
    qsend,
    qrecv,
    kfull,
    vfull,
    kloc,
    vloc,
    oloc,
    lloc,
    osend,
    orecv,
    ssend,
    srecv,
    tsend,
    tz,
    tpl,
    tfin,
    wbuf,
    acc,
    load_sem,
    fresh_sem,
    own_sem,
    kv_recv,
    a2a_send,
    sib_send,
    row_send,
    q_send,
    q_recv,
    o_send,
    o_recv,
    s_send,
    s_recv,
    tz_send,
    tz_recv,
    tp_send,
    tp_recv,
    tf_send,
    tf_recv,
):
    A = GROUPS
    B = n // A
    rows = img_qkv.shape[0]
    trows = txt_qkv.shape[0]
    me = lax.axis_index("patch")
    a = me // B
    b = lax.rem(me, B)
    core = lax.rem(b, 2)
    sib = b + 1 - 2 * core
    chip = b // 2
    chips = B // 2

    def over(k):
        return lax.rem(a + k, A)

    def row_peer(j):
        return 2 * lax.rem(chip + j, chips) + core

    def remote(src, dst, send, recv, to_a, to_b):
        return pltpu.make_async_remote_copy(
            src_ref=src,
            dst_ref=dst,
            send_sem=send,
            recv_sem=recv,
            device_id={"patch": to_a * B + to_b},
            device_id_type=pl.DeviceIdType.MESH,
        )

    def got(dst, sem):
        remote(dst, dst, sem, sem, a, sib).wait_recv()

    started = []

    def go(copy):
        copy.start()
        started.append(copy)

    loads = [
        pltpu.make_async_copy(src, dst, load_sem.at[i])
        for i, (src, dst) in enumerate(
            (
                (img_qkv_hbm, img_qkv),
                (img_gain_hbm, img_gain),
                (txt_qkv_hbm, txt_qkv),
                (txt_gain_hbm, txt_gain),
                (txt_mask_hbm, txt_mask),
                (txt_w_hbm, txt_w),
                (txt_hidden_hbm, txt_hidden),
                (txt_gate_hbm, txt_gate),
                (img_hidden_hbm, img_hidden),
                (img_gate_hbm, img_gate),
                (w_hbm, wbuf),
            )
        )
    ]
    for load in loads[:5]:
        load.start()

    barrier = pltpu.get_barrier_semaphore()
    for k in range(1, A):
        pl.semaphore_signal(
            barrier, inc=1, device_id={"patch": over(k) * B + b}, device_id_type=pl.DeviceIdType.MESH
        )
    for k in range(1, B):
        pl.semaphore_signal(
            barrier,
            inc=1,
            device_id={"patch": a * B + lax.rem(b + k, B)},
            device_id_type=pl.DeviceIdType.MESH,
        )
    def cols(group):
        return pl.ds(pl.multiple_of(group * GW, GW), GW)

    def slot(bb, aa):
        return bb * A + aa

    mine = slot(b, a)
    own_copy = pltpu.make_async_copy(stale.at[:, :, cols(a)], kvbuf.at[mine], own_sem)
    own_copy.start()
    pl.semaphore_wait(barrier, A + B - 2)
    def exchange(which):
        for k in range(1, A):
            go(
                remote(
                    stale.at[which, :, cols(over(k))],
                    kvbuf.at[mine, which],
                    a2a_send.at[k, which],
                    kv_recv.at[mine, which],
                    over(k),
                    b,
                )
            )
        return started[-(A - 1) :]

    def left(copies):
        for copy in copies:
            copy.wait_send()
        started[:] = [copy for copy in started if all(copy is not c for c in copies)]

    def spread(k, which):
        s = slot(b, over(k))
        part = kvbuf.at[s, which]
        for j in range(1, chips):
            go(
                remote(
                    part,
                    part,
                    row_send.at[k * chips + j, which],
                    kv_recv.at[s, which],
                    a,
                    row_peer(j),
                )
            )
        go(remote(part, part, sib_send.at[k, which], kv_recv.at[s, which], a, sib))

    def forward(k, which):
        for j in range(1, chips):
            s = slot(row_peer(j), over(k))
            part = kvbuf.at[s, which]
            got(part, kv_recv.at[s, which])
            go(remote(part, part, sib_send.at[j * A + k, which], kv_recv.at[s, which], a, sib))

    keys_away = exchange(0)
    own_copy.wait()
    spread(0, 0)
    spread(0, 1)
    for load in loads[5:10]:
        load.start()
    for load in loads[:2]:
        load.wait()

    for h in range(HEADS):
        c = slice(h * HD, (h + 1) * HD)
        qsend[:, c] = normed(img_qkv[:, c], img_gain[0:1, :])
    qrecv[a] = qsend[:, cols(a)]

    left(keys_away)
    values_away = exchange(1)

    for load in loads[2:5]:
        load.wait()
    pad = jnp.zeros((LOC - rows - trows, HD), F32)
    for h in range(HEADS):
        c = slice(h * HD, (h + 1) * HD)
        ck = slice(HW + h * HD, HW + (h + 1) * HD)
        cv = slice(2 * HW + h * HD, 2 * HW + (h + 1) * HD)
        own = normed(img_qkv[:, ck], img_gain[1:2, :])
        fresh[0, :, c] = own
        value = img_qkv[:, cv]
        fresh[1, :, c] = value
        text = normed(txt_qkv[:, ck], txt_gain[1:2, :])
        kloc[:, c] = jnp.concatenate([text.astype(F32), own.astype(F32), pad]).astype(BF16)
        vloc[:, c] = jnp.concatenate(
            [txt_qkv[:, cv].astype(F32), value.astype(F32), pad]
        ).astype(BF16)

    keep_fresh = pltpu.make_async_copy(fresh, fresh_hbm, fresh_sem)
    keep_fresh.start()

    forward(0, 0)
    forward(0, 1)
    for k in range(1, A):
        s = slot(b, over(k))
        got(kvbuf.at[s, 0], kv_recv.at[s, 0])
        spread(k, 0)

    lane = lax.broadcasted_iota(jnp.int32, (1, LOC), 1)
    wide_mask[...] = jnp.zeros((1, LOC), jnp.int32)
    wide_mask[:, :trows] = txt_mask[...]
    in_text = wide_mask[...] == 1
    in_img = (lane >= trows) & (lane < trows + rows)
    bias_img = jnp.where(in_img | in_text, 0.0, LOW)
    bias_txt = jnp.where(in_img | (in_text & (me == 0)), 0.0, LOW)

    for g in range(GROUPS):
        logs = []
        for j in range(PER):
            h = g * PER + j
            c = slice(h * HD, (h + 1) * HD)
            query = normed(txt_qkv[:, c], txt_gain[0:1, :])
            mixed, log = soft(nt(query, kloc[:, c]) + bias_txt, vloc[:, c])
            tsend[g, :, j * HD : (j + 1) * HD] = mixed.astype(BF16)
            logs.append(log)
        tsend[g, :, GW:] = pack(logs, trows)

    def only(condition, act):
        if B == A:
            act()
        else:
            pl.when(condition)(act)

    def beside(k):
        return lax.rem(b + k, B)

    def text_part(k):
        t = beside(k)
        return remote(tsend.at[t], tpl.at[b], tp_send.at[k], tp_recv.at[b], a, t)

    def text_group(k):
        return remote(tz.at[a], tz.at[a], tz_send.at[k], tz_recv.at[a], over(k), b)

    def text_final(k):
        return remote(tfin.at[b], tfin.at[b], tf_send.at[k], tf_recv.at[b], a, beside(k))

    for k in range(1, B):
        only(beside(k) < A, lambda k=k: text_part(k).start())

    def own_part():
        tpl[b] = tsend[b]

    only(b < A, own_part)

    def merge_text(blocks, where):
        logs = []
        for j in range(PER):
            c = slice(j * HD, (j + 1) * HD)
            mixed, log = merge(
                [(blk[:, c].astype(F32), unpack(blk, j, trows)) for blk in blocks]
            )
            where(c, mixed.astype(BF16))
            logs.append(log)
        return logs

    def over_plane():
        for k in range(1, B):
            got(tpl.at[beside(k)], tp_recv.at[beside(k)])

        def put(c, mixed):
            tz[a, :, c] = mixed

        tz[a, :, GW:] = pack(merge_text([tpl[i] for i in range(B)], put), trows)
        for k in range(1, A):
            text_group(k).start()

    def over_z():
        for k in range(1, A):
            got(tz.at[over(k)], tz_recv.at[over(k)])

        def put(c, mixed):
            tfin[b, :, c] = mixed

        merge_text([tz[i] for i in range(A)], put)
        for k in range(1, B):
            text_final(k).start()

    def local_heads(first, last):
        stats = lloc[...] if first else jnp.zeros((rows, HD), F32)
        spot = lanes_of(rows)
        for h in range(first, last):
            c = slice(h * HD, (h + 1) * HD)
            mixed, log = soft(nt(qsend[:, c], kloc[:, c]) + bias_img, vloc[:, c])
            oloc[:, c] = mixed
            stats = jnp.where(spot == h, log, stats)
        lloc[...] = stats

    def assemble(bb):
        for i in range(A // 2):
            s = slot(bb, 2 * i)
            at = pl.ds(pl.multiple_of(s * rows, 2 * rows), 2 * rows)
            for which, full in ((0, kfull), (1, vfull)):
                full[at, :] = jnp.concatenate(
                    [kvbuf[s, which].astype(F32), kvbuf[s + 1, which].astype(F32)]
                ).astype(BF16)

    step = HEADS // (A - 1)
    left(values_away)
    for k in range(1, A):
        go(
            remote(
                qsend.at[:, cols(over(k))], qrecv.at[a], q_send.at[k], q_recv.at[a], over(k), b
            )
        )
    queries_away = started[-(A - 1) :]
    for k in range(1, A):
        s = slot(b, over(k))
        got(kvbuf.at[s, 1], kv_recv.at[s, 1])
        spread(k, 1)
    left(queries_away)
    only(b < A, over_plane)
    loads[10].start()
    for k in range(1, A):
        forward(k, 0)
        local_heads((k - 1) * step, k * step)
    for k in range(1, A):
        forward(k, 1)

    for j in range(chips):
        assemble(row_peer(j) if j else b)

    for j in range(chips):
        bb = 2 * lax.rem(chip + j, chips) + 1 - core
        for k in range(A):
            s = slot(bb, over(k))
            got(kvbuf.at[s, 0], kv_recv.at[s, 0])
            got(kvbuf.at[s, 1], kv_recv.at[s, 1])
        assemble(bb)
    for k in range(1, A):
        got(qrecv.at[over(k)], q_recv.at[over(k)])

    place = lax.broadcasted_iota(jnp.int32, (1, n * rows), 1)

    def attend(group, out, stats):
        start = slot(b, group) * rows
        bias = jnp.where((place >= start) & (place < start + rows), LOW, 0.0)
        logs = []
        for j in range(PER):
            c = slice(j * HD, (j + 1) * HD)
            mixed, log = soft(nt(qrecv[group, :, c], kfull[:, c]) + bias, vfull[:, c])
            out[:, c] = mixed.astype(BF16)
            logs.append(log)
        stats[...] = pack_across(logs, rows)

    for k in range(1, A):
        attend(over(k), osend.at[k], ssend.at[k])
        go(remote(ssend.at[k], srecv.at[a], s_send.at[k], s_recv.at[a], over(k), b))
        go(remote(osend.at[k], orecv.at[a], o_send.at[k], o_recv.at[a], over(k), b))
        if k == 1:
            only(b < A, over_z)
    attend(a, orecv.at[a], srecv.at[a])

    for load in loads[5:]:
        load.wait()
    width = img_hidden.shape[1]
    tile = width // 4
    spot = lanes_of(rows)
    for k in range(A):
        group = over(A - k) if k else a
        if k == A - 1:
            for i in range(1, B):
                t = beside(i)
                only(t < A, lambda t=t: got(tfin.at[t], tf_recv.at[t]))
            text = jnp.concatenate([tfin[i] for i in range(A)], axis=1)
            txt_out[...] = (
                txt_hidden[...].astype(F32) + txt_gate[...] * nt(text, txt_w[...])
            ).astype(BF16)
        if k:
            got(orecv.at[group], o_recv.at[group])
            got(srecv.at[group], s_recv.at[group])
        block = orecv[group]
        stats = unpack_across(srecv[group], rows)
        base = oloc[:, cols(group)]
        attn = []
        for j in range(PER):
            c = slice(j * HD, (j + 1) * HD)
            log = jnp.sum(
                jnp.where(spot == group * PER + j, lloc[...], 0.0), axis=-1, keepdims=True
            )
            mixed, _ = merge(
                [(block[:, c].astype(F32), joined(stats, j, rows)), (base[:, c], log)]
            )
            attn.append(mixed.astype(BF16))
        attn = jnp.concatenate(attn, axis=1)
        for t in range(4):
            c = slice(t * tile, (t + 1) * tile)
            part = jnp.dot(attn, wbuf[cols(group), c], preferred_element_type=F32)
            if k:
                part = acc[:, c] + part
            if k < A - 1:
                acc[:, c] = part
            else:
                img_out[:, c] = (
                    img_hidden[:, c].astype(F32) + img_gate[:, c] * part
                ).astype(BF16)

    def text_left():
        for k in range(1, A):
            text_group(k).wait_send()
        for k in range(1, B):
            text_final(k).wait_send()

    for k in range(1, B):
        only(beside(k) < A, lambda k=k: text_part(k).wait_send())
    only(b < A, text_left)
    keep_fresh.wait()
    for copy in started:
        copy.wait_send()


def keep(count, *refs):
    sources, results, held = (refs[i * count : (i + 1) * count] for i in range(3))
    in_sem, out_sem = refs[3 * count :]
    loads = [
        pltpu.make_async_copy(sources[i], held[i], in_sem.at[i]) for i in range(count)
    ]
    stores = [
        pltpu.make_async_copy(held[i], results[i], out_sem.at[i]) for i in range(count)
    ]
    for load in loads:
        load.start()
    for load, store in zip(loads, stores):
        load.wait()
        store.start()
    for store in stores:
        store.wait()


def body(
    img_hidden,
    img_qkv,
    stale_kv,
    txt_hidden,
    txt_qkv,
    txt_mask,
    img_qk_gain,
    txt_qk_gain,
    img_gate,
    txt_gate,
    img_out_w,
    txt_out_w,
):
    n = lax.axis_size("patch")
    A = GROUPS
    B = n // A
    rows, width = img_hidden.shape
    trows = txt_qkv.shape[0]
    vmem = pl.BlockSpec(memory_space=pltpu.VMEM)
    dma = pltpu.SemaphoreType.DMA
    results = pl.pallas_call(
        functools.partial(kernel, n),
        out_shape=(
            jax.ShapeDtypeStruct(img_hidden.shape, BF16),
            jax.ShapeDtypeStruct(txt_hidden.shape, BF16),
            jax.ShapeDtypeStruct(stale_kv.shape, BF16),
        ),
        in_specs=[pl.BlockSpec(memory_space=pltpu.HBM)] * 12,
        out_specs=(vmem, vmem, pl.BlockSpec(memory_space=pltpu.HBM)),
        scratch_shapes=[
            pltpu.VMEM(img_hidden.shape, BF16),
            pltpu.VMEM(img_qkv.shape, BF16),
            pltpu.VMEM(txt_hidden.shape, BF16),
            pltpu.VMEM(txt_qkv.shape, BF16),
            pltpu.VMEM((1, trows), jnp.int32),
            pltpu.VMEM(img_qk_gain.shape, F32),
            pltpu.VMEM(txt_qk_gain.shape, F32),
            pltpu.VMEM((1, width), F32),
            pltpu.VMEM((1, txt_gate.shape[0]), F32),
            pltpu.VMEM(txt_out_w.shape[::-1], BF16),
            pltpu.VMEM((1, LOC), jnp.int32),
            pltpu.VMEM(stale_kv.shape, BF16),
            pltpu.VMEM((n, 2, rows, GW), BF16),
            pltpu.VMEM((rows, HW), BF16),
            pltpu.VMEM((A, rows, GW), BF16),
            pltpu.VMEM((n * rows, GW), BF16),
            pltpu.VMEM((n * rows, GW), BF16),
            pltpu.VMEM((LOC, HW), BF16),
            pltpu.VMEM((LOC, HW), BF16),
            pltpu.VMEM((rows, HW), F32),
            pltpu.VMEM((rows, HD), F32),
            pltpu.VMEM((A, rows, GW), BF16),
            pltpu.VMEM((A, rows, GW), BF16),
            pltpu.VMEM((A, STAT, HD), BF16),
            pltpu.VMEM((A, STAT, HD), BF16),
            pltpu.VMEM((A, trows, GW + HD), BF16),
            pltpu.VMEM((A, trows, GW + HD), BF16),
            pltpu.VMEM((B, trows, GW + HD), BF16),
            pltpu.VMEM((A, trows, GW), BF16),
            pltpu.VMEM(img_out_w.shape, BF16),
            pltpu.VMEM((rows, width), F32),
            dma((11,)),
            dma,
            dma,
            dma((n, 2)),
            dma((A, 2)),
            dma((n, 2)),
            dma((n, 2)),
            dma((A,)),
            dma((A,)),
            dma((A,)),
            dma((A,)),
            dma((A,)),
            dma((A,)),
            dma((A,)),
            dma((A,)),
            dma((B,)),
            dma((B,)),
            dma((B,)),
            dma((A,)),
        ],
        compiler_params=pltpu.CompilerParams(
            collective_id=0, has_side_effects=True, vmem_limit_bytes=64 * 1024 * 1024
        ),
        name="joint_attention",
    )(
        img_hidden,
        img_qkv,
        stale_kv,
        txt_hidden,
        txt_qkv,
        txt_mask.reshape(1, -1),
        img_qk_gain,
        txt_qk_gain,
        img_gate.reshape(1, -1),
        txt_gate.reshape(1, -1),
        img_out_w,
        txt_out_w.T,
    )
    hbm = pl.BlockSpec(memory_space=pltpu.HBM)
    return pl.pallas_call(
        functools.partial(keep, 3),
        out_shape=tuple(jax.ShapeDtypeStruct(x.shape, x.dtype) for x in results),
        in_specs=[hbm] * 3,
        out_specs=(hbm,) * 3,
        scratch_shapes=[pltpu.VMEM(x.shape, x.dtype) for x in results] + [dma((3,)), dma((3,))],
        compiler_params=pltpu.CompilerParams(vmem_limit_bytes=64 * 1024 * 1024),
        name="keep_results",
    )(*results)


def solution(mesh):
    placed = (
        P(("group", "patch"), None),
        P(("group", "patch"), None),
        P(None, ("group", "patch"), None),
        P("group", "patch"),
        P("group", None),
        P("group"),
        P(),
        P(),
        P("group"),
        P(("group", "patch")),
        P(),
        P(None, "patch"),
    )
    return jax.shard_map(
        body,
        mesh=mesh,
        in_specs=placed,
        out_specs=(
            P(("group", "patch"), None),
            P("group", "patch"),
            P(None, ("group", "patch"), None),
        ),
        check_vma=False,
    )
```
